768 devices in a mesh: ia: 16 (over z_hi, y), ja: 6 (over z_lo), ka: 8 (over x, core).
Axes of the slice: x: 4, y: 8, z: 12 (z_hi: 2, z_lo: 6; z = z_hi * 6 + z_lo), core: 2. Of those that a mesh axis runs over, the one named last changes fastest.
Arguments:
- flow_state: float32 [128, 5, 96, 1024], P('ia', None, 'ja', 'ka'), may hold values from -1.5 to 7, as said below
- mode_shapes: float32 [64, 128, 96], P('ka', 'ia', 'ja'), may hold values from -1 to 1
- modal_coords: float32 [2, 64], replicated, may hold values from -0.5 to 0.5
- wall_mask: int32 [128, 96], P('ia', 'ja'), may hold values 0 or 1
Outputs:
- new_state: float32 [128, 5, 96, 1024], P('ia', None, 'ja', 'ka')
- gen_force: float32 [64], P('ka')
The draws below stay inside these ranges and needn't reach their ends.
Inputs may be any that keep to these rules, and one draw needn't show every extreme that they name: `flow_state`: in every cell the density lies between 0.5 and 2 and the pressure 0.4 (energy - 0.5 |momentum|^2 / density) between 0.4 and 2.
All inputs are finite; a program needn't handle non-finite values. No bound on the sum of `wall_mask` on one device may be relied on, other than what follows from the above.
Results may differ from the reference program's by a relative error of at most 0.0003.
Values sent between devices are 32-bit elements; how exact they have to be, the bound alone decides.
A program may use at most 32 MiB of HBM per device.

```python
import math
import jax
import jax.numpy as jnp
from jax import lax

NMODE = 64
NI = 128
NJ = 96
NK = 1024


def draw_flow_state(key, part):
    key_density = jax.random.fold_in(key, 11)
    key_speed = jax.random.fold_in(key, 12)
    key_pressure = jax.random.fold_in(key, 13)
    density = jnp.exp(jax.random.uniform(key_density, (NI, NJ, NK), jnp.float32, math.log(0.5), math.log(2.0)))
    velocity = jax.random.uniform(key_speed, (3, NI, NJ, NK), jnp.float32, -0.6, 0.6)
    pressure = jnp.exp(jax.random.uniform(key_pressure, (NI, NJ, NK), jnp.float32, math.log(0.4), math.log(2.0)))
    energy = pressure / 0.4 + 0.5 * density * (velocity[0] * velocity[0] + velocity[1] * velocity[1] + velocity[2] * velocity[2])
    return jnp.stack([density, density * velocity[0], density * velocity[1], density * velocity[2], energy], axis=1)


def touch_ends(entries, stream_key, low, largest):
    extent = entries.shape
    place = [jax.random.randint(jax.random.fold_in(stream_key, axis), (), 0, extent[axis]) for axis in range(len(extent))]
    entries = entries.at[tuple(place)].set(low)
    longest = extent.index(max(extent))
    place[longest] = (place[longest] + 1) % extent[longest]
    return entries.at[tuple(place)].set(largest)


def shard_levels(stream_key, dims, pieces, low, high):
    def one(position, blocks):
        draws = jax.random.uniform(jax.random.fold_in(jax.random.fold_in(stream_key, 6), position), (blocks,), jnp.float32, low / len(pieces), high / len(pieces))
        return jnp.repeat(jnp.exp(draws), dims[position] // blocks).reshape((-1,) + (1,) * (len(dims) - position - 1))

    level = one(*pieces[0])
    for cut in pieces[1:]:
        level = level * one(*cut)
    return level


def setup_inputs(seed: int = 0) -> dict:
    arg_keys = jax.random.split(jax.random.key(seed), 5)
    flow_state = draw_flow_state(jax.random.fold_in(arg_keys[4], 71), 0)
    mode_shapes = jnp.clip(jax.random.uniform(arg_keys[1], (NMODE, NI, NJ), jnp.float32, -1.0, 1.0) * shard_levels(arg_keys[1], (NMODE, NI, NJ), ((0, 8), (1, 16), (2, 6)), -0.4, 0.0), -1.0, 1.0)
    modal_coords = jnp.clip(jax.random.uniform(arg_keys[2], (2, NMODE), jnp.float32, -0.5, 0.5), -0.5, 0.5)
    wall_mask = touch_ends((jax.random.randint(arg_keys[3], (NI, NJ), 0, 3) < 2).astype(jnp.int32), jax.random.fold_in(arg_keys[3], 1), 0, 1)
    return dict(flow_state=flow_state, mode_shapes=mode_shapes, modal_coords=modal_coords, wall_mask=wall_mask)


HEAT_RATIO = 1.4
SECTION_STEP = 0.2
STRAIN = 0.25
FAR_PRESSURE = 0.8
FAR_STATE = (1.0, 0.6, 0.0, 0.0, 0.8)

def primitives(conserved):
    density = conserved[:, 0]
    along_x = conserved[:, 1] / density
    along_y = conserved[:, 2] / density
    along_z = conserved[:, 3] / density
    pressure = (HEAT_RATIO - 1.0) * (conserved[:, 4] - 0.5 * density * (along_x * along_x + along_y * along_y + along_z * along_z))
    return jnp.stack([density, along_x, along_y, along_z, pressure], axis=1)

def minmod(first, second):
    return 0.5 * (jnp.sign(first) + jnp.sign(second)) * jnp.minimum(jnp.abs(first), jnp.abs(second))

def euler_flux(prim, component, grid_speed):
    density = prim[:, 0]
    along_x = prim[:, 1]
    along_y = prim[:, 2]
    along_z = prim[:, 3]
    pressure = prim[:, 4]
    normal_speed = prim[:, component] - grid_speed
    energy = pressure / (HEAT_RATIO - 1.0) + 0.5 * density * (along_x * along_x + along_y * along_y + along_z * along_z)
    conserved = [density, density * along_x, density * along_y, density * along_z, energy]
    fluxes = [quantity * normal_speed for quantity in conserved]
    fluxes[component] = fluxes[component] + pressure
    fluxes[4] = fluxes[4] + pressure * prim[:, component]
    wave = jnp.abs(normal_speed) + jnp.sqrt(HEAT_RATIO * pressure / density)
    return (jnp.stack(conserved, axis=1), jnp.stack(fluxes, axis=1), wave)

def face_fluxes(prim, direction, component, grid_speed):
    length = prim.shape[direction]
    cell_a = lax.slice_in_dim(prim, 0, length - 3, axis=direction)
    cell_b = lax.slice_in_dim(prim, 1, length - 2, axis=direction)
    cell_c = lax.slice_in_dim(prim, 2, length - 1, axis=direction)
    cell_d = lax.slice_in_dim(prim, 3, length, axis=direction)
    left_state = cell_b + 0.5 * minmod(cell_b - cell_a, cell_c - cell_b)
    right_state = cell_c - 0.5 * minmod(cell_c - cell_b, cell_d - cell_c)
    left_cons, left_flux, left_wave = euler_flux(left_state, component, grid_speed)
    right_cons, right_flux, right_wave = euler_flux(right_state, component, grid_speed)
    return 0.5 * (left_flux + right_flux) - 0.5 * jnp.maximum(left_wave, right_wave)[:, None] * (right_cons - left_cons)

def ghost_rims(center, wall_speed, mask_row, far):
    count, width_j, width_k = (center.shape[0], center.shape[2], center.shape[3])
    far_b = far[None, :, None, None]
    side = jnp.broadcast_to(far_b, (count, 5, 2, width_k))
    padded = jnp.concatenate([side, center, side], axis=2)
    upper_rim = jnp.broadcast_to(far_b, (count, 5, width_j + 4, 2))
    mirror = center[..., 0:2][..., ::-1]
    reflected = 2.0 * wall_speed[:, :, None] - mirror[:, 3]
    mirror = jnp.concatenate([mirror[:, 0:3], reflected[:, None], mirror[:, 4:5]], axis=1)
    lower_rim = jnp.where(mask_row[:, None, :, None] == 1, mirror, far_b)
    lower_side = jnp.broadcast_to(far_b, (count, 5, 2, 2))
    lower_rim = jnp.concatenate([lower_side, lower_rim, lower_side], axis=2)
    return jnp.concatenate([lower_rim, padded, upper_rim], axis=3)

def reference(flow_state, mode_shapes, modal_coords, wall_mask):
    highest = lax.Precision.HIGHEST
    far = jnp.array(FAR_STATE, jnp.float32)
    displacement = jnp.einsum('m,mij->ij', modal_coords[0], mode_shapes, precision=highest)
    wall_speed = jnp.einsum('m,mij->ij', modal_coords[1], mode_shapes, precision=highest)
    wall_prim = primitives(flow_state[:, :, :, 0:1])
    wall_load = jnp.where(wall_mask == 1, wall_prim[:, 4, :, 0] - FAR_PRESSURE, 0.0)
    gen_force = jnp.einsum('mij,ij->m', mode_shapes, wall_load, precision=highest) / math.sqrt(NI * NJ)
    face_pos = jnp.arange(NK + 1, dtype=jnp.int32).astype(jnp.float32) / NK
    face_weight = (1.0 - face_pos) ** 2
    cell_pos = (jnp.arange(NK, dtype=jnp.int32).astype(jnp.float32) + 0.5) / NK

    def one_plane(plane_index):
        indices = (plane_index + jnp.arange(-2, 3, dtype=jnp.int32)).astype(jnp.int32)
        clamped = jnp.clip(indices, 0, NI - 1).astype(jnp.int32)
        slab_prim = primitives(jnp.take(flow_state, clamped, axis=0))
        inside = (indices >= 0) & (indices < NI)
        slab_prim = jnp.where(inside[:, None, None, None], slab_prim, far[None, :, None, None])
        flux_i = face_fluxes(slab_prim, 0, 1, 0.0)
        speed_row = lax.dynamic_slice_in_dim(wall_speed, plane_index, 1, 0)
        mask_row = lax.dynamic_slice_in_dim(wall_mask, plane_index, 1, 0)
        shift_row = lax.dynamic_slice_in_dim(displacement, plane_index, 1, 0)
        padded = ghost_rims(slab_prim[2:3], speed_row, mask_row, far)
        flux_j = face_fluxes(padded[:, :, :, 2:-2], 2, 2, 0.0)
        grid_speed = face_weight[None, None, :] * speed_row[:, :, None]
        flux_k = face_fluxes(padded[:, :, 2:-2, :], 3, 3, grid_speed)
        residual = flux_i[1:] - flux_i[:-1] + (flux_j[:, :, 1:] - flux_j[:, :, :-1]) + (flux_k[..., 1:] - flux_k[..., :-1])
        volume_ratio = jnp.exp(-STRAIN * (1.0 - cell_pos)[None, None, :] * shift_row[:, :, None])
        current = lax.dynamic_slice_in_dim(flow_state, plane_index, 1, 0)
        return (current - SECTION_STEP * residual / volume_ratio[:, None])[0]
    new_state = lax.map(one_plane, jnp.arange(NI, dtype=jnp.int32))
    return (new_state, gen_force)
```

```python
import functools
import math

import jax
import jax.numpy as jnp
from jax import lax
from jax.experimental import pallas as pl
from jax.experimental.pallas import tpu as pltpu
from jax.sharding import PartitionSpec as P

MESH = pl.DeviceIdType.MESH
SECTION_STEP = 0.2
STRAIN = 0.25
FAR_PRESSURE = 0.8
FAR_STATE = (1.0, 0.6, 0.0, 0.0, 0.8)


def primitives(block):
    density, mom_x, mom_y, mom_z, energy = block
    inverse = 1.0 / density
    pressure = 0.4 * (energy - 0.5 * (mom_x * mom_x + mom_y * mom_y + mom_z * mom_z) * inverse)
    return [density, mom_x * inverse, mom_y * inverse, mom_z * inverse, pressure]


def minmod(x, y):
    return jnp.maximum(jnp.minimum(x, jnp.maximum(y, 0.0)), jnp.minimum(y, 0.0))


def side_flux(state, component, grid_speed):
    density, along_x, along_y, along_z, pressure = state
    own = state[component]
    normal = own if grid_speed is None else own - grid_speed
    mom = [density * along_x, density * along_y, density * along_z]
    energy = 2.5 * pressure + 0.5 * (mom[0] * along_x + mom[1] * along_y + mom[2] * along_z)
    conserved = [density] + mom + [energy]
    flux = [quantity * normal for quantity in conserved]
    flux[component] = flux[component] + pressure
    flux[4] = flux[4] + pressure * own
    wave = jnp.abs(normal) + math.sqrt(1.4) * pressure * lax.rsqrt(pressure * density)
    return conserved, flux, wave


def faces(a, b, c, d, component, grid_speed=None):
    left, right = [], []
    for wa, wb, wc, wd in zip(a, b, c, d):
        middle = wc - wb
        left.append(wb + 0.5 * minmod(wb - wa, middle))
        right.append(wc - 0.5 * minmod(middle, wd - wc))
    left_cons, left_flux, left_wave = side_flux(left, component, grid_speed)
    right_cons, right_flux, right_wave = side_flux(right, component, grid_speed)
    wave = jnp.maximum(left_wave, right_wave)
    return [
        lf + rf - wave * (rc - lc)
        for lf, rf, lc, rc in zip(left_flux, right_flux, left_cons, right_cons)
    ]


def section(
    sizes, flow, shapes, coords, mask, new, force,
    fv, sv, mv, prim, raw_i, raw_j, send_k, halo_k, edge_k, planes, planes_in,
    s_own, l_own, s_all, l_all, g_own, g_in, flux_i,
    local_sem, send_sem, recv_sem, many_sem,
):
    ni, nj, nk = sizes
    ia, ja, ka = lax.axis_index("ia"), lax.axis_index("ja"), lax.axis_index("ka")
    li, lj, lk = flow.shape[0], flow.shape[2], flow.shape[3]
    modes = shapes.shape[0]
    columns = ni * nj
    column = ia * nj + ja
    is_root = column == 0
    total_k = nk * lk

    in_flow = pltpu.make_async_copy(flow, fv, local_sem.at[0])
    in_shapes = pltpu.make_async_copy(shapes, sv, local_sem.at[1])
    in_mask = pltpu.make_async_copy(mask, mv, local_sem.at[2])
    in_flow.start()
    in_shapes.start()
    in_mask.start()

    barrier = pltpu.get_barrier_semaphore()

    def greet(where):
        pl.semaphore_signal(barrier, inc=1, device_id=where, device_id_type=MESH)

    @pl.when(is_root)
    def _():
        @pl.loop(1, columns)
        def _(c):
            greet({"ia": c // nj, "ja": lax.rem(c, nj)})

        @pl.when(ka > 0)
        def _():
            @pl.loop(0, columns)
            def _(c):
                greet({"ia": c // nj, "ja": lax.rem(c, nj), "ka": 0})

    beside = [
        (ia > 0, {"ia": jnp.maximum(ia - 1, 0)}),
        (ia < ni - 1, {"ia": jnp.minimum(ia + 1, ni - 1)}),
        (ja > 0, {"ja": jnp.maximum(ja - 1, 0)}),
        (ja < nj - 1, {"ja": jnp.minimum(ja + 1, nj - 1)}),
    ]
    expected = nk - 1
    for there, where in beside:
        pl.when(there)(functools.partial(greet, where))
        expected = expected + there.astype(jnp.int32)
    for o in range(1, nk):
        greet({"ka": lax.rem(ka + o, nk)})
    expected = expected + jnp.where(is_root, 0, 1) + jnp.where(ka == 0, nk - 1, 0)

    lane = lax.broadcasted_iota(jnp.int32, (8, 128), 1)

    in_shapes.wait()
    in_mask.wait()
    packed = jnp.zeros((li, 128), jnp.float32)
    disp = jnp.zeros((li, lj), jnp.float32)
    speed = jnp.zeros((li, lj), jnp.float32)
    zeros = jnp.zeros((li, 128 - lj), jnp.float32)
    for m in range(modes):
        one = sv[m]
        wide = jnp.concatenate([one, zeros], axis=1)
        packed = packed + (pltpu.roll(wide, lj * m, 1) if m else wide)
        disp = disp + coords[0, ka * modes + m] * one
        speed = speed + coords[1, ka * modes + m] * one
    s_own[...] = packed
    planes[...] = jnp.concatenate([disp, speed, jnp.zeros((li, 128 - 2 * lj), jnp.float32)], axis=1)

    in_flow.wait()

    @pl.when(ka == 0)
    def _():
        lane_t = lax.broadcasted_iota(jnp.int32, (lj, 128), 1)
        turned = jnp.zeros((lj, 128), jnp.float32)
        for i in range(li):
            p = primitives([fv[i, c, :, 0:1] for c in range(5)])[4]
            turned = turned + jnp.where(lax.rem(lane_t, li) == i, p - FAR_PRESSURE, 0.0)
        flat = jnp.concatenate([turned] * (128 // lj), axis=0).T[0:li]
        keep = jnp.concatenate([mv[...]] * (128 // lj), axis=1)
        l_own[...] = jnp.where(keep == 1, flat, 0.0)

    pl.semaphore_wait(barrier, expected)

    def to_root(src, dst, sem_index, recv, where):
        return pltpu.make_async_remote_copy(
            src_ref=src, dst_ref=dst, send_sem=send_sem.at[sem_index], recv_sem=recv,
            device_id=where, device_id_type=MESH,
        )

    root_here = {"ia": 0, "ja": 0}
    load_copies = [
        to_root(l_own, l_all.at[column], 8 + o, many_sem.at[1], {"ia": 0, "ja": 0, "ka": o})
        for o in range(nk)
    ]
    shape_copy = to_root(s_own, s_all.at[column], 7, many_sem.at[0], root_here)

    @pl.when(ka == 0)
    def _():
        for o, copy in enumerate(load_copies):
            if o:
                copy.start()
            else:
                pl.when(~is_root)(copy.start)

    pl.when(~is_root)(shape_copy.start)

    @pl.when(is_root)
    def _():
        s_all[0] = s_own[...]

        @pl.when(ka == 0)
        def _():
            l_all[0] = l_own[...]

    def halo(src, dst, index, where):
        return pltpu.make_async_remote_copy(
            src_ref=src, dst_ref=dst, send_sem=send_sem.at[index], recv_sem=recv_sem.at[index],
            device_id=where, device_id_type=MESH,
        )

    (has_i0, to_i0), (has_i1, to_i1), (has_j0, to_j0), (has_j1, to_j1) = beside
    has_k0, has_k1 = ka > 0, ka < nk - 1
    copies = [
        (halo(flow.at[li - 2 : li], raw_i.at[0], 0, to_i1), has_i1, has_i0),
        (halo(flow.at[0:2], raw_i.at[1], 1, to_i0), has_i0, has_i1),
        (halo(flow.at[:, :, lj - 8 : lj], raw_j.at[0], 2, to_j1), has_j1, has_j0),
        (halo(flow.at[:, :, 0:8], raw_j.at[1], 3, to_j0), has_j0, has_j1),
        (halo(send_k.at[0], halo_k.at[0], 4, {"ka": jnp.minimum(ka + 1, nk - 1)}), has_k1, has_k0),
        (halo(send_k.at[1], halo_k.at[1], 5, {"ka": jnp.maximum(ka - 1, 0)}), has_k0, has_k1),
    ]
    for copy, sends, _ in copies[0:4]:
        pl.when(sends)(copy.start)

    plane_copies = [
        pltpu.make_async_remote_copy(
            src_ref=planes, dst_ref=planes_in.at[o - 1], send_sem=send_sem.at[15 + o],
            recv_sem=many_sem.at[2], device_id={"ka": lax.rem(ka + o, nk)}, device_id_type=MESH,
        )
        for o in range(1, nk)
    ]
    for copy in plane_copies:
        copy.start()

    lane_j = lax.broadcasted_iota(jnp.int32, (lj, 128), 1)
    send_k[...] = jnp.zeros_like(send_k)

    @pl.loop(0, li)
    def _(i):
        here = lane_j // 2 == i
        for c, w in enumerate(primitives([fv[i, c] for c in range(5)])):
            prim[i + 2, c, 8 : 8 + lj] = w
            send_k[0, c] = jnp.where(here, pltpu.roll(w, 2 * i + 2, 1), send_k[0, c])
            send_k[1, c] = jnp.where(here, pltpu.roll(w, 2 * i, 1), send_k[1, c])

    for copy, sends, _ in copies[4:6]:
        pl.when(sends)(copy.start)

    def far(shape, c):
        return jnp.full(shape, FAR_STATE[c], jnp.float32)

    pltpu.make_async_copy(planes_in, planes_in, many_sem.at[2]).wait()
    total = planes[...]
    for o in range(nk - 1):
        total = total + planes_in[o]
    wall = mv[...].astype(jnp.float32)
    wall = jnp.concatenate([jnp.zeros((li, 2 * lj), jnp.float32), wall, jnp.zeros((li, 128 - 3 * lj), jnp.float32)], axis=1)
    turned = jnp.concatenate([total + wall, jnp.zeros((128 - li, 128), jnp.float32)], axis=0).T

    for side, (base, (copy, _, gets)) in enumerate(zip((0, li + 2), copies[0:2])):

        @pl.when(gets)
        def _(side=side, base=base, copy=copy):
            copy.wait_recv()
            for r in range(2):
                for c, w in enumerate(primitives([raw_i[side, r, c] for c in range(5)])):
                    prim[base + r, c, 8 : 8 + lj] = w

        @pl.when(~gets)
        def _(base=base):
            for r in range(2):
                for c in range(5):
                    prim[base + r, c, 8 : 8 + lj] = far((lj, lk), c)

    for side, (base, (copy, _, gets)) in enumerate(zip((0, 8 + lj), copies[2:4])):

        @pl.when(gets)
        def _(side=side, base=base, copy=copy):
            copy.wait_recv()

            @pl.loop(0, li)
            def _(i):
                for c, w in enumerate(primitives([raw_j[side, i, c] for c in range(5)])):
                    prim[i + 2, c, base : base + 8] = w

        @pl.when(~gets)
        def _(base=base):
            @pl.loop(0, li)
            def _(i):
                for c in range(5):
                    prim[i + 2, c, base : base + 8] = far((8, lk), c)

    pl.when(has_k0)(copies[4][0].wait_recv)
    pl.when(has_k1)(copies[5][0].wait_recv)

    @pl.when(~has_k0)
    def _():
        halo_k[0] = jnp.zeros(halo_k.shape[1:], jnp.float32)

    @pl.when(~has_k1)
    def _():
        for c in range(5):
            halo_k[1, c] = far((lj, 128), c)

    first = ka * lk
    own_pair = [send_k[0, c] for c in range(5)]
    next_pair = [halo_k[1, c] for c in range(5)]
    last_weight = (1.0 - (first + lk).astype(jnp.float32) / total_k) ** 2
    speed_pairs = jnp.zeros((lj, 128), jnp.float32)
    for i in range(li):
        speed_pairs = jnp.where(lane_j // 2 == i, turned[lj : 2 * lj, i : i + 1], speed_pairs)
    last = faces(
        own_pair,
        [pltpu.roll(w, 127, 1) for w in own_pair],
        next_pair,
        [pltpu.roll(w, 127, 1) for w in next_pair],
        3,
        last_weight * speed_pairs,
    )
    for c in range(5):
        edge_k[c] = last[c]

    def cells(i, lo, rows):
        return [prim[i, c, lo : lo + rows] for c in range(5)]

    def along_i(i):
        return faces(cells(i, 8, lj), cells(i + 1, 8, lj), cells(i + 2, 8, lj), cells(i + 3, 8, lj), 1)

    for c, w in enumerate(along_i(0)):
        flux_i[c] = w
    at_wall = ka == 0
    lane_f = (first + lane_j).astype(jnp.float32)
    face_weight = (1.0 - lane_f / total_k) ** 2
    cell_weight = STRAIN * (1.0 - (lane_f + 0.5) / total_k)
    first_lane, pair_lane, last_lane = lane_j < 1, lane_j < 2, lane_j == lk - 1
    column_lane = lax.broadcasted_iota(jnp.int32, (3 * lj, 128), 1)

    @pl.loop(0, li)
    def _(i):
        column_i = jnp.sum(jnp.where(column_lane == i, turned[0 : 3 * lj], 0.0), axis=1, keepdims=True)
        disp_i = column_i[0:lj]
        speed_i = jnp.broadcast_to(column_i[lj : 2 * lj], (lj, 128))
        solid = jnp.broadcast_to(column_i[2 * lj : 3 * lj], (lj, 128)) > 0.5

        upper = along_i(i + 1)
        residual = []
        for c in range(5):
            residual.append(upper[c] - flux_i[c])
            flux_i[c] = upper[c]

        rows = lj + 8
        flux_j = faces(cells(i + 2, 6, rows), cells(i + 2, 7, rows), cells(i + 2, 8, rows), cells(i + 2, 9, rows), 2)
        residual = [r + (f[1 : lj + 1] - f[0:lj]) for r, f in zip(residual, flux_j)]

        below2, below, above = [], [], []
        own = cells(i + 2, 8, lj)
        for c, w in enumerate(own):
            up = jnp.where(last_lane, pltpu.roll(halo_k[1, c], lk - 1 - 2 * i, 1), pltpu.roll(w, lk - 1, 1))
            down = pltpu.roll(w, 1, 1)
            mirror2 = jnp.where(first_lane, up, down)
            mirror1 = w
            if c == 3:
                mirror2 = 2.0 * speed_i - mirror2
                mirror1 = 2.0 * speed_i - mirror1
            mirror2 = jnp.where(solid, mirror2, FAR_STATE[c])
            mirror1 = jnp.where(solid, mirror1, FAR_STATE[c])
            ghost = halo_k[0, c]
            ghost2 = jnp.where(at_wall, mirror2, pltpu.roll(ghost, lax.rem(lk - 2 * i, lk), 1))
            ghost1 = jnp.where(at_wall, mirror1, pltpu.roll(ghost, lk - 1 - 2 * i, 1))
            below2.append(jnp.where(pair_lane, ghost2, pltpu.roll(w, 2, 1)))
            below.append(jnp.where(first_lane, ghost1, down))
            above.append(up)
        flux_k = faces(below2, below, own, above, 3, face_weight * speed_i)
        growth = (-0.5 * SECTION_STEP) * jnp.exp(cell_weight * disp_i)
        for c, f in enumerate(flux_k):
            end = pltpu.roll(edge_k[c], lk - 1 - 2 * i, 1)
            high = jnp.where(last_lane, end, pltpu.roll(f, lk - 1, 1))
            new[i, c] = fv[i, c] + growth * (residual[c] + (high - f))

    @pl.when(is_root)
    def _():
        others = s_all.at[1:columns]
        pltpu.make_async_copy(others, others, many_sem.at[0]).wait()

        @pl.when(ka == 0)
        def _():
            loads = l_all.at[1:columns]
            pltpu.make_async_copy(loads, loads, many_sem.at[1]).wait()

        @pl.when(ka > 0)
        def _():
            pltpu.make_async_copy(l_all, l_all, many_sem.at[1]).wait()

        g_own[...] = jnp.sum(s_all[...] * l_all[...], axis=0)

        @pl.loop(1, columns)
        def _(c):
            pltpu.make_async_remote_copy(
                src_ref=g_own, dst_ref=g_in, send_sem=many_sem.at[4], recv_sem=many_sem.at[3],
                device_id={"ia": c // nj, "ja": lax.rem(c, nj)}, device_id_type=MESH,
            ).start()

        force[...] = g_own[...]

    @pl.when(~is_root)
    def _():
        pltpu.make_async_copy(g_in, g_in, many_sem.at[3]).wait()
        force[...] = g_in[...]

    for copy, sends, _ in copies:
        pl.when(sends)(copy.wait_send)
    for copy in plane_copies:
        copy.wait_send()
    pl.when(~is_root)(shape_copy.wait_send)

    @pl.when(ka == 0)
    def _():
        for o, copy in enumerate(load_copies):
            if o:
                copy.wait_send()
            else:
                pl.when(~is_root)(copy.wait_send)

    @pl.when(is_root)
    def _():
        others = s_all.at[1:columns]
        pltpu.make_async_copy(others, others, many_sem.at[4]).wait()


def finish(scale, new, partial, out, force, sem):
    copy = pltpu.make_async_copy(new, out, sem)
    copy.start()
    group = partial.shape[1] // 8
    row = lax.broadcasted_iota(jnp.int32, (8, 128), 0)
    lane = lax.broadcasted_iota(jnp.int32, (8, 128), 1)
    summed = jnp.sum(partial[...], axis=0, keepdims=True)
    each = jnp.sum(jnp.where(lane // group == row, summed, 0.0), axis=1, keepdims=True)
    force[...] = jnp.sum(jnp.where(lane == row, each, 0.0), axis=0, keepdims=True)[:, 0:8] * scale
    copy.wait()


def solution(mesh):
    sizes = (mesh.shape["ia"], mesh.shape["ja"], mesh.shape["ka"])
    ni, nj, nk = sizes

    def local(flow_state, mode_shapes, modal_coords, wall_mask):
        li, _, lj, lk = flow_state.shape
        modes = mode_shapes.shape[0]
        f32 = jnp.float32
        tile = pltpu.VMEM((8, 128), f32)
        vmem = pl.BlockSpec(memory_space=pltpu.VMEM)
        hbm = pl.BlockSpec(memory_space=pltpu.HBM)
        free = pl.BlockSpec(memory_space=pl.ANY)
        new, partial = pl.pallas_call(
            functools.partial(section, sizes),
            out_shape=(
                jax.ShapeDtypeStruct(flow_state.shape, f32),
                jax.ShapeDtypeStruct((8, 128), f32),
            ),
            in_specs=[hbm, hbm, pl.BlockSpec(memory_space=pltpu.SMEM), hbm],
            out_specs=(vmem, vmem),
            scratch_shapes=[
                pltpu.VMEM(flow_state.shape, f32),
                pltpu.VMEM(mode_shapes.shape, f32),
                pltpu.VMEM(wall_mask.shape, jnp.int32),
                pltpu.VMEM((li + 4, 5, lj + 24, lk), f32),
                pltpu.VMEM((2, 2, 5, lj, lk), f32),
                pltpu.VMEM((2, li, 5, 8, lk), f32),
                pltpu.VMEM((2, 5, lj, 128), f32),
                pltpu.VMEM((2, 5, lj, 128), f32),
                pltpu.VMEM((5, lj, 128), f32),
                tile,
                pltpu.VMEM((nk - 1, 8, 128), f32),
                tile,
                tile,
                pltpu.VMEM((ni * nj, 8, 128), f32),
                pltpu.VMEM((ni * nj, 8, 128), f32),
                tile,
                tile,
                pltpu.VMEM((5, lj, lk), f32),
                pltpu.SemaphoreType.DMA((3,)),
                pltpu.SemaphoreType.DMA((15 + nk,)),
                pltpu.SemaphoreType.DMA((6,)),
                pltpu.SemaphoreType.DMA((5,)),
            ],
            compiler_params=pltpu.CompilerParams(
                collective_id=0, has_side_effects=True, vmem_limit_bytes=32 * 1024 * 1024
            ),
            name="section",
        )(flow_state, mode_shapes, modal_coords, wall_mask)
        out, force = pl.pallas_call(
            functools.partial(finish, 1.0 / math.sqrt(ni * li * nj * lj)),
            out_shape=(
                jax.ShapeDtypeStruct(flow_state.shape, f32),
                jax.ShapeDtypeStruct((1, modes), f32),
            ),
            in_specs=[free, vmem],
            out_specs=(hbm, vmem),
            scratch_shapes=[pltpu.SemaphoreType.DMA],
            name="finish",
        )(new, partial)
        return (out, force.reshape(modes))

    return jax.shard_map(
        local,
        mesh=mesh,
        in_specs=(P("ia", None, "ja", "ka"), P("ka", "ia", "ja"), P(), P("ia", "ja")),
        out_specs=(P("ia", None, "ja", "ka"), P("ka")),
        check_vma=False,
    )
```

```python
import functools
import math

import jax
import jax.numpy as jnp
from jax import lax
from jax.experimental import pallas as pl
from jax.experimental.pallas import tpu as pltpu
from jax.sharding import PartitionSpec as P

MESH = pl.DeviceIdType.MESH
SECTION_STEP = 0.2
STRAIN = 0.25
FAR_PRESSURE = 0.8
FAR_STATE = (1.0, 0.6, 0.0, 0.0, 0.8)


def primitives(block):
    density, mom_x, mom_y, mom_z, energy = block
    inverse = 1.0 / density
    pressure = 0.4 * (energy - 0.5 * (mom_x * mom_x + mom_y * mom_y + mom_z * mom_z) * inverse)
    return [density, mom_x * inverse, mom_y * inverse, mom_z * inverse, pressure]


def minmod(x, y):
    return jnp.maximum(jnp.minimum(x, jnp.maximum(y, 0.0)), jnp.minimum(y, 0.0))


def side_flux(state, component, grid_speed):
    density, along_x, along_y, along_z, pressure = state
    own = state[component]
    normal = own if grid_speed is None else own - grid_speed
    mom = [density * along_x, density * along_y, density * along_z]
    energy = 2.5 * pressure + 0.5 * (mom[0] * along_x + mom[1] * along_y + mom[2] * along_z)
    conserved = [density] + mom + [energy]
    flux = [quantity * normal for quantity in conserved]
    flux[component] = flux[component] + pressure
    flux[4] = flux[4] + pressure * own
    wave = jnp.abs(normal) + math.sqrt(1.4) * pressure * lax.rsqrt(pressure * density)
    return conserved, flux, wave


def faces(a, b, c, d, component, grid_speed=None):
    left, right = [], []
    for wa, wb, wc, wd in zip(a, b, c, d):
        middle = wc - wb
        left.append(wb + 0.5 * minmod(wb - wa, middle))
        right.append(wc - 0.5 * minmod(middle, wd - wc))
    left_cons, left_flux, left_wave = side_flux(left, component, grid_speed)
    right_cons, right_flux, right_wave = side_flux(right, component, grid_speed)
    wave = jnp.maximum(left_wave, right_wave)
    return [
        lf + rf - wave * (rc - lc)
        for lf, rf, lc, rc in zip(left_flux, right_flux, left_cons, right_cons)
    ]


def section(
    sizes, flow, shapes, coords_in, mask, new, force,
    fv, sv, mv, coords, prim, raw_i, raw_j, send_k, halo_k, edge_k, planes, planes_in,
    s_own, l_own, s_all, l_all, g_own, g_in, flux_i,
    local_sem, send_sem, recv_sem, many_sem,
):
    ni, nj, nk = sizes
    ia, ja, ka = lax.axis_index("ia"), lax.axis_index("ja"), lax.axis_index("ka")
    li, lj, lk = flow.shape[0], flow.shape[2], flow.shape[3]
    modes = shapes.shape[0]
    columns = ni * nj
    column = ia * nj + ja
    is_root = column == 0
    total_k = nk * lk

    in_flow = pltpu.make_async_copy(flow, fv, local_sem.at[0])
    in_shapes = pltpu.make_async_copy(shapes, sv, local_sem.at[1])
    in_mask = pltpu.make_async_copy(mask, mv, local_sem.at[2])
    in_coords = pltpu.make_async_copy(coords_in, coords, local_sem.at[3])
    in_flow.start()
    in_shapes.start()
    in_mask.start()
    in_coords.start()

    barrier = pltpu.get_barrier_semaphore()

    def greet(where):
        pl.semaphore_signal(barrier, inc=1, device_id=where, device_id_type=MESH)

    @pl.when(is_root)
    def _():
        @pl.loop(1, columns)
        def _(c):
            greet({"ia": c // nj, "ja": lax.rem(c, nj)})

        @pl.when(ka > 0)
        def _():
            @pl.loop(0, columns)
            def _(c):
                greet({"ia": c // nj, "ja": lax.rem(c, nj), "ka": 0})

    beside = [
        (ia > 0, {"ia": jnp.maximum(ia - 1, 0)}),
        (ia < ni - 1, {"ia": jnp.minimum(ia + 1, ni - 1)}),
        (ja > 0, {"ja": jnp.maximum(ja - 1, 0)}),
        (ja < nj - 1, {"ja": jnp.minimum(ja + 1, nj - 1)}),
    ]
    expected = nk - 1
    for there, where in beside:
        pl.when(there)(functools.partial(greet, where))
        expected = expected + there.astype(jnp.int32)
    for o in range(1, nk):
        greet({"ka": lax.rem(ka + o, nk)})
    expected = expected + jnp.where(is_root, 0, 1) + jnp.where(ka == 0, nk - 1, 0)

    lane = lax.broadcasted_iota(jnp.int32, (8, 128), 1)

    in_shapes.wait()
    in_mask.wait()
    in_coords.wait()
    packed = jnp.zeros((modes, 128), jnp.float32)
    disp = jnp.zeros((li, lj), jnp.float32)
    speed = jnp.zeros((li, lj), jnp.float32)
    zeros = jnp.zeros((modes, 128 - lj), jnp.float32)
    for i in range(li):
        wide = jnp.concatenate([sv[:, i, :], zeros], axis=1)
        packed = packed + (pltpu.roll(wide, lj * i, 1) if i else wide)
    for m in range(modes):
        one = sv[m]
        disp = disp + coords[0, ka * modes + m] * one
        speed = speed + coords[1, ka * modes + m] * one
    s_own[...] = packed
    planes[...] = jnp.concatenate([disp, speed, jnp.zeros((li, 128 - 2 * lj), jnp.float32)], axis=1)

    in_flow.wait()

    @pl.when(ka == 0)
    def _():
        lane_t = lax.broadcasted_iota(jnp.int32, (lj, 128), 1)
        turned = jnp.zeros((lj, 128), jnp.float32)
        for i in range(li):
            p = primitives([fv[i, c, :, 0:1] for c in range(5)])[4]
            turned = turned + jnp.where(lax.rem(lane_t, li) == i, p - FAR_PRESSURE, 0.0)
        flat = jnp.concatenate([turned] * (128 // lj), axis=0).T[0:li]
        keep = jnp.concatenate([mv[...]] * (128 // lj), axis=1)
        own_row = lane // lj == lax.broadcasted_iota(jnp.int32, (8, 128), 0)
        l_own[...] = jnp.sum(jnp.where(own_row & (keep == 1), flat, 0.0), axis=0, keepdims=True)

    pl.semaphore_wait(barrier, expected)

    def to_root(src, dst, sem_index, recv, where):
        return pltpu.make_async_remote_copy(
            src_ref=src, dst_ref=dst, send_sem=send_sem.at[sem_index], recv_sem=recv,
            device_id=where, device_id_type=MESH,
        )

    root_here = {"ia": 0, "ja": 0}
    load_copies = [
        to_root(l_own, l_all.at[column], 8 + o, many_sem.at[1], {"ia": 0, "ja": 0, "ka": o})
        for o in range(nk)
    ]
    shape_copy = to_root(s_own, s_all.at[column], 7, many_sem.at[0], root_here)

    @pl.when(ka == 0)
    def _():
        for o, copy in enumerate(load_copies):
            if o:
                copy.start()
            else:
                pl.when(~is_root)(copy.start)

    pl.when(~is_root)(shape_copy.start)

    @pl.when(is_root)
    def _():
        s_all[0] = s_own[...]

        @pl.when(ka == 0)
        def _():
            l_all[0] = l_own[...]

    def halo(src, dst, index, where):
        return pltpu.make_async_remote_copy(
            src_ref=src, dst_ref=dst, send_sem=send_sem.at[index], recv_sem=recv_sem.at[index],
            device_id=where, device_id_type=MESH,
        )

    (has_i0, to_i0), (has_i1, to_i1), (has_j0, to_j0), (has_j1, to_j1) = beside
    has_k0, has_k1 = ka > 0, ka < nk - 1
    copies = [
        (halo(flow.at[li - 2 : li], raw_i.at[0], 0, to_i1), has_i1, has_i0),
        (halo(flow.at[0:2], raw_i.at[1], 1, to_i0), has_i0, has_i1),
        (halo(flow.at[:, :, lj - 8 : lj], raw_j.at[0], 2, to_j1), has_j1, has_j0),
        (halo(flow.at[:, :, 0:8], raw_j.at[1], 3, to_j0), has_j0, has_j1),
        (halo(send_k.at[0], halo_k.at[0], 4, {"ka": jnp.minimum(ka + 1, nk - 1)}), has_k1, has_k0),
        (halo(send_k.at[1], halo_k.at[1], 5, {"ka": jnp.maximum(ka - 1, 0)}), has_k0, has_k1),
    ]
    for copy, sends, _ in copies[0:4]:
        pl.when(sends)(copy.start)

    plane_copies = [
        pltpu.make_async_remote_copy(
            src_ref=planes, dst_ref=planes_in.at[o - 1], send_sem=send_sem.at[15 + o],
            recv_sem=many_sem.at[2], device_id={"ka": lax.rem(ka + o, nk)}, device_id_type=MESH,
        )
        for o in range(1, nk)
    ]
    for copy in plane_copies:
        copy.start()

    lane_j = lax.broadcasted_iota(jnp.int32, (lj, 128), 1)
    send_k[...] = jnp.zeros_like(send_k)

    @pl.loop(0, li)
    def _(i):
        here = lane_j // 2 == i
        for c, w in enumerate(primitives([fv[i, c] for c in range(5)])):
            prim[i + 2, c, 8 : 8 + lj] = w
            send_k[0, c] = jnp.where(here, pltpu.roll(w, 2 * i + 2, 1), send_k[0, c])
            send_k[1, c] = jnp.where(here, pltpu.roll(w, 2 * i, 1), send_k[1, c])

    for copy, sends, _ in copies[4:6]:
        pl.when(sends)(copy.start)

    def far(shape, c):
        return jnp.full(shape, FAR_STATE[c], jnp.float32)

    pltpu.make_async_copy(planes_in, planes_in, many_sem.at[2]).wait()
    total = planes[...]
    for o in range(nk - 1):
        total = total + planes_in[o]
    wall = mv[...].astype(jnp.float32)
    wall = jnp.concatenate([jnp.zeros((li, 2 * lj), jnp.float32), wall, jnp.zeros((li, 128 - 3 * lj), jnp.float32)], axis=1)
    turned = jnp.concatenate([total + wall, jnp.zeros((128 - li, 128), jnp.float32)], axis=0).T

    for side, (base, (copy, _, gets)) in enumerate(zip((0, li + 2), copies[0:2])):

        @pl.when(gets)
        def _(side=side, base=base, copy=copy):
            copy.wait_recv()
            for r in range(2):
                for c, w in enumerate(primitives([raw_i[side, r, c] for c in range(5)])):
                    prim[base + r, c, 8 : 8 + lj] = w

        @pl.when(~gets)
        def _(base=base):
            for r in range(2):
                for c in range(5):
                    prim[base + r, c, 8 : 8 + lj] = far((lj, lk), c)

    for side, (base, (copy, _, gets)) in enumerate(zip((0, 8 + lj), copies[2:4])):

        @pl.when(gets)
        def _(side=side, base=base, copy=copy):
            copy.wait_recv()

            @pl.loop(0, li)
            def _(i):
                for c, w in enumerate(primitives([raw_j[side, i, c] for c in range(5)])):
                    prim[i + 2, c, base : base + 8] = w

        @pl.when(~gets)
        def _(base=base):
            @pl.loop(0, li)
            def _(i):
                for c in range(5):
                    prim[i + 2, c, base : base + 8] = far((8, lk), c)

    pl.when(has_k0)(copies[4][0].wait_recv)
    pl.when(has_k1)(copies[5][0].wait_recv)

    @pl.when(~has_k0)
    def _():
        halo_k[0] = jnp.zeros(halo_k.shape[1:], jnp.float32)

    @pl.when(~has_k1)
    def _():
        for c in range(5):
            halo_k[1, c] = far((lj, 128), c)

    first = ka * lk
    own_pair = [send_k[0, c] for c in range(5)]
    next_pair = [halo_k[1, c] for c in range(5)]
    last_weight = (1.0 - (first + lk).astype(jnp.float32) / total_k) ** 2
    speed_pairs = jnp.zeros((lj, 128), jnp.float32)
    for i in range(li):
        speed_pairs = jnp.where(lane_j // 2 == i, turned[lj : 2 * lj, i : i + 1], speed_pairs)
    last = faces(
        own_pair,
        [pltpu.roll(w, 127, 1) for w in own_pair],
        next_pair,
        [pltpu.roll(w, 127, 1) for w in next_pair],
        3,
        last_weight * speed_pairs,
    )
    for c in range(5):
        edge_k[c] = last[c]

    def cells(i, lo, rows):
        return [prim[i, c, lo : lo + rows] for c in range(5)]

    def along_i(i):
        return faces(cells(i, 8, lj), cells(i + 1, 8, lj), cells(i + 2, 8, lj), cells(i + 3, 8, lj), 1)

    for c, w in enumerate(along_i(0)):
        flux_i[c] = w
    at_wall = ka == 0
    lane_f = (first + lane_j).astype(jnp.float32)
    face_weight = (1.0 - lane_f / total_k) ** 2
    cell_weight = STRAIN * (1.0 - (lane_f + 0.5) / total_k)
    first_lane, pair_lane, last_lane = lane_j < 1, lane_j < 2, lane_j == lk - 1
    column_lane = lax.broadcasted_iota(jnp.int32, (3 * lj, 128), 1)

    @pl.loop(0, li)
    def _(i):
        column_i = jnp.sum(jnp.where(column_lane == i, turned[0 : 3 * lj], 0.0), axis=1, keepdims=True)
        disp_i = column_i[0:lj]
        speed_i = jnp.broadcast_to(column_i[lj : 2 * lj], (lj, 128))
        solid = jnp.broadcast_to(column_i[2 * lj : 3 * lj], (lj, 128)) > 0.5

        upper = along_i(i + 1)
        residual = []
        for c in range(5):
            residual.append(upper[c] - flux_i[c])
            flux_i[c] = upper[c]

        rows = lj + 8
        flux_j = faces(cells(i + 2, 6, rows), cells(i + 2, 7, rows), cells(i + 2, 8, rows), cells(i + 2, 9, rows), 2)
        residual = [r + (f[1 : lj + 1] - f[0:lj]) for r, f in zip(residual, flux_j)]

        below2, below, above = [], [], []
        own = cells(i + 2, 8, lj)
        for c, w in enumerate(own):
            up = jnp.where(last_lane, pltpu.roll(halo_k[1, c], lk - 1 - 2 * i, 1), pltpu.roll(w, lk - 1, 1))
            down = pltpu.roll(w, 1, 1)
            mirror2 = jnp.where(first_lane, up, down)
            mirror1 = w
            if c == 3:
                mirror2 = 2.0 * speed_i - mirror2
                mirror1 = 2.0 * speed_i - mirror1
            mirror2 = jnp.where(solid, mirror2, FAR_STATE[c])
            mirror1 = jnp.where(solid, mirror1, FAR_STATE[c])
            ghost = halo_k[0, c]
            ghost2 = jnp.where(at_wall, mirror2, pltpu.roll(ghost, lax.rem(lk - 2 * i, lk), 1))
            ghost1 = jnp.where(at_wall, mirror1, pltpu.roll(ghost, lk - 1 - 2 * i, 1))
            below2.append(jnp.where(pair_lane, ghost2, pltpu.roll(w, 2, 1)))
            below.append(jnp.where(first_lane, ghost1, down))
            above.append(up)
        flux_k = faces(below2, below, own, above, 3, face_weight * speed_i)
        growth = (-0.5 * SECTION_STEP) * jnp.exp(cell_weight * disp_i)
        for c, f in enumerate(flux_k):
            end = pltpu.roll(edge_k[c], lk - 1 - 2 * i, 1)
            high = jnp.where(last_lane, end, pltpu.roll(f, lk - 1, 1))
            new[i, c] = fv[i, c] + growth * (residual[c] + (high - f))

    @pl.when(is_root)
    def _():
        others = s_all.at[1:columns]
        pltpu.make_async_copy(others, others, many_sem.at[0]).wait()

        @pl.when(ka == 0)
        def _():
            loads = l_all.at[1:columns]
            pltpu.make_async_copy(loads, loads, many_sem.at[1]).wait()

        @pl.when(ka > 0)
        def _():
            pltpu.make_async_copy(l_all, l_all, many_sem.at[1]).wait()

        summed = jnp.sum(s_all[...] * l_all[...], axis=0)
        each = jnp.sum(summed, axis=1, keepdims=True)
        row = lax.broadcasted_iota(jnp.int32, (8, 128), 0)
        g_own[...] = jnp.sum(jnp.where(lane == row, each, 0.0), axis=0, keepdims=True)

        @pl.loop(1, columns)
        def _(c):
            pltpu.make_async_remote_copy(
                src_ref=g_own, dst_ref=g_in, send_sem=many_sem.at[4], recv_sem=many_sem.at[3],
                device_id={"ia": c // nj, "ja": lax.rem(c, nj)}, device_id_type=MESH,
            ).start()

        force[...] = g_own[...]

    @pl.when(~is_root)
    def _():
        pltpu.make_async_copy(g_in, g_in, many_sem.at[3]).wait()
        force[...] = g_in[...]

    for copy, sends, _ in copies:
        pl.when(sends)(copy.wait_send)
    for copy in plane_copies:
        copy.wait_send()
    pl.when(~is_root)(shape_copy.wait_send)

    @pl.when(ka == 0)
    def _():
        for o, copy in enumerate(load_copies):
            if o:
                copy.wait_send()
            else:
                pl.when(~is_root)(copy.wait_send)

    @pl.when(is_root)
    def _():
        others = l_all.at[1:columns]
        pltpu.make_async_copy(others, others, many_sem.at[4]).wait()


def finish(scale, new, partial, out, force, sem):
    copy = pltpu.make_async_copy(new, out, sem)
    copy.start()
    force[...] = partial[:, 0 : force.shape[1]] * scale
    copy.wait()


def solution(mesh):
    sizes = (mesh.shape["ia"], mesh.shape["ja"], mesh.shape["ka"])
    ni, nj, nk = sizes

    def local(flow_state, mode_shapes, modal_coords, wall_mask):
        li, _, lj, lk = flow_state.shape
        modes = mode_shapes.shape[0]
        f32 = jnp.float32
        tile = pltpu.VMEM((8, 128), f32)
        row = pltpu.VMEM((1, 128), f32)
        vmem = pl.BlockSpec(memory_space=pltpu.VMEM)
        hbm = pl.BlockSpec(memory_space=pltpu.HBM)
        held = functools.partial(pltpu.with_memory_space_constraint, memory_space=pltpu.HBM)
        new, partial = pl.pallas_call(
            functools.partial(section, sizes),
            out_shape=(pltpu.VMEM(flow_state.shape, f32), pltpu.VMEM((1, 128), f32)),
            in_specs=[hbm, hbm, hbm, hbm],
            out_specs=(vmem, vmem),
            scratch_shapes=[
                pltpu.VMEM(flow_state.shape, f32),
                pltpu.VMEM(mode_shapes.shape, f32),
                pltpu.VMEM(wall_mask.shape, jnp.int32),
                pltpu.SMEM(modal_coords.shape, f32),
                pltpu.VMEM((li + 4, 5, lj + 24, lk), f32),
                pltpu.VMEM((2, 2, 5, lj, lk), f32),
                pltpu.VMEM((2, li, 5, 8, lk), f32),
                pltpu.VMEM((2, 5, lj, 128), f32),
                pltpu.VMEM((2, 5, lj, 128), f32),
                pltpu.VMEM((5, lj, 128), f32),
                tile,
                pltpu.VMEM((nk - 1, 8, 128), f32),
                tile,
                row,
                pltpu.VMEM((ni * nj, 8, 128), f32),
                pltpu.VMEM((ni * nj, 1, 128), f32),
                row,
                row,
                pltpu.VMEM((5, lj, lk), f32),
                pltpu.SemaphoreType.DMA((4,)),
                pltpu.SemaphoreType.DMA((15 + nk,)),
                pltpu.SemaphoreType.DMA((6,)),
                pltpu.SemaphoreType.DMA((5,)),
            ],
            compiler_params=pltpu.CompilerParams(
                collective_id=0, has_side_effects=True, vmem_limit_bytes=32 * 1024 * 1024
            ),
            name="section",
        )(held(flow_state), held(mode_shapes), held(modal_coords), held(wall_mask))
        out, force = pl.pallas_call(
            functools.partial(finish, 1.0 / math.sqrt(ni * li * nj * lj)),
            out_shape=(
                jax.ShapeDtypeStruct(flow_state.shape, f32),
                jax.ShapeDtypeStruct((1, modes), f32),
            ),
            in_specs=[vmem, vmem],
            out_specs=(hbm, vmem),
            scratch_shapes=[pltpu.SemaphoreType.DMA],
            compiler_params=pltpu.CompilerParams(vmem_limit_bytes=8 * 1024 * 1024),
            name="finish",
        )(new, partial)
        return (out, force.reshape(modes))

    return jax.shard_map(
        local,
        mesh=mesh,
        in_specs=(P("ia", None, "ja", "ka"), P("ka", "ia", "ja"), P(), P("ia", "ja")),
        out_specs=(P("ia", None, "ja", "ka"), P("ka")),
        check_vma=False,
    )
```

```python
import functools
import math

import jax
import jax.numpy as jnp
from jax import lax
from jax.experimental import pallas as pl
from jax.experimental.pallas import tpu as pltpu
from jax.sharding import PartitionSpec as P

MESH = pl.DeviceIdType.MESH
SECTION_STEP = 0.2
STRAIN = 0.25
FAR_PRESSURE = 0.8
ROOT_WALL = (1, 0)
ROOT = (0, 0)
FAR_STATE = (1.0, 0.6, 0.0, 0.0, 0.8)


def primitives(block):
    density, mom_x, mom_y, mom_z, energy = block
    inverse = 1.0 / density
    pressure = 0.4 * (energy - 0.5 * (mom_x * mom_x + mom_y * mom_y + mom_z * mom_z) * inverse)
    return [density, mom_x * inverse, mom_y * inverse, mom_z * inverse, pressure]


def minmod(x, y):
    return jnp.maximum(jnp.minimum(x, jnp.maximum(y, 0.0)), jnp.minimum(y, 0.0))


def side_flux(state, component, grid_speed):
    density, along_x, along_y, along_z, pressure = state
    own = state[component]
    normal = own if grid_speed is None else own - grid_speed
    mom = [density * along_x, density * along_y, density * along_z]
    energy = 2.5 * pressure + 0.5 * (mom[0] * along_x + mom[1] * along_y + mom[2] * along_z)
    conserved = [density] + mom + [energy]
    flux = [quantity * normal for quantity in conserved]
    flux[component] = flux[component] + pressure
    flux[4] = flux[4] + pressure * own
    wave = jnp.abs(normal) + math.sqrt(1.4) * pressure * lax.rsqrt(pressure * density)
    return conserved, flux, wave


def faces(a, b, c, d, component, grid_speed=None):
    left, right = [], []
    for wa, wb, wc, wd in zip(a, b, c, d):
        middle = wc - wb
        left.append(wb + 0.5 * minmod(wb - wa, middle))
        right.append(wc - 0.5 * minmod(middle, wd - wc))
    left_cons, left_flux, left_wave = side_flux(left, component, grid_speed)
    right_cons, right_flux, right_wave = side_flux(right, component, grid_speed)
    wave = jnp.maximum(left_wave, right_wave)
    return [
        lf + rf - wave * (rc - lc)
        for lf, rf, lc, rc in zip(left_flux, right_flux, left_cons, right_cons)
    ]


def section(
    sizes, flow, shapes, coords_in, mask, new, force,
    fv, sv, mv, coords, prim, raw_i, raw_j, send_k, halo_k, edge_k, planes, planes_in,
    s_own, l_own, s_all, l_all, g_own, flux_i,
    local_sem, send_sem, recv_sem, many_sem, column_sem,
):
    ni, nj, nk = sizes
    ia, ja, ka = lax.axis_index("ia"), lax.axis_index("ja"), lax.axis_index("ka")
    li, lj, lk = flow.shape[0], flow.shape[2], flow.shape[3]
    modes = shapes.shape[0]
    columns = ni * nj
    lines = 8 if ni % 8 == 0 else ni
    root_of = [(i % lines, j % nj) for i, j in [ROOT_WALL] + [ROOT] * (nk - 1)]
    root_ia = jnp.where(ka == 0, root_of[0][0], root_of[-1][0])
    root_ja = jnp.where(ka == 0, root_of[0][1], root_of[-1][1])
    column = ia * nj + ja
    is_root = column == root_ia * nj + root_ja
    total_k = nk * lk

    in_flow = pltpu.make_async_copy(flow, fv, local_sem.at[0])
    in_shapes = pltpu.make_async_copy(shapes, sv, local_sem.at[1])
    in_mask = pltpu.make_async_copy(mask, mv, local_sem.at[2])
    in_coords = pltpu.make_async_copy(coords_in, coords, local_sem.at[3])
    in_flow.start()
    in_shapes.start()
    in_mask.start()
    in_coords.start()

    barrier = pltpu.get_barrier_semaphore()

    def greet(where):
        pl.semaphore_signal(barrier, inc=1, device_id=where, device_id_type=MESH)

    @pl.when(is_root)
    def _():
        def next_to(c):
            c = lax.rem(2 * columns - c + column, columns)
            return {"ia": c // nj, "ja": lax.rem(c, nj)}

        @pl.when(ka > 0)
        def _():
            @pl.loop(0, columns)
            def _(c):
                greet({**next_to(c), "ka": 0})

        @pl.loop(1, columns)
        def _(c):
            greet(next_to(c))

    beside = [
        (ia > 0, {"ia": jnp.maximum(ia - 1, 0)}),
        (ia < ni - 1, {"ia": jnp.minimum(ia + 1, ni - 1)}),
        (ja > 0, {"ja": jnp.maximum(ja - 1, 0)}),
        (ja < nj - 1, {"ja": jnp.minimum(ja + 1, nj - 1)}),
    ]
    expected = jnp.where(is_root, 0, 1) + jnp.where(ka == 0, nk - 1, 0)
    for there, where in beside:
        pl.when(there)(functools.partial(greet, where))
        expected = expected + there.astype(jnp.int32)
    lead = nk // 2
    leads = ka == lead
    pl.when(~leads)(functools.partial(greet, {"ka": lead}))
    expected = expected + jnp.where(leads, nk - 1, 0)

    lane = lax.broadcasted_iota(jnp.int32, (8, 128), 1)

    in_shapes.wait()
    in_mask.wait()
    in_coords.wait()
    packed = jnp.zeros((modes, 128), jnp.float32)
    disp = jnp.zeros((li, lj), jnp.float32)
    speed = jnp.zeros((li, lj), jnp.float32)
    zeros = jnp.zeros((modes, 128 - lj), jnp.float32)
    for i in range(li):
        wide = jnp.concatenate([sv[:, i, :], zeros], axis=1)
        packed = packed + (pltpu.roll(wide, lj * i, 1) if i else wide)
    for m in range(modes):
        one = sv[m]
        disp = disp + coords[0, ka * modes + m] * one
        speed = speed + coords[1, ka * modes + m] * one
    s_own[...] = packed
    planes[...] = jnp.concatenate([disp, speed, jnp.zeros((li, 128 - 2 * lj), jnp.float32)], axis=1)

    in_flow.wait()

    @pl.when(ka == 0)
    def _():
        lane_t = lax.broadcasted_iota(jnp.int32, (lj, 128), 1)
        turned = jnp.zeros((lj, 128), jnp.float32)
        for i in range(li):
            p = primitives([fv[i, c, :, 0:1] for c in range(5)])[4]
            turned = turned + jnp.where(lax.rem(lane_t, li) == i, p - FAR_PRESSURE, 0.0)
        flat = jnp.concatenate([turned] * (128 // lj), axis=0).T[0:li]
        keep = jnp.concatenate([mv[...]] * (128 // lj), axis=1)
        own_row = lane // lj == lax.broadcasted_iota(jnp.int32, (8, 128), 0)
        l_own[...] = jnp.sum(jnp.where(own_row & (keep == 1), flat, 0.0), axis=0, keepdims=True)

    pl.semaphore_wait(barrier, expected)

    @pl.when(leads)
    def _():
        for o in range(1, nk):
            pl.semaphore_signal(
                column_sem, inc=1, device_id={"ka": lax.rem(ka + o, nk)}, device_id_type=MESH
            )

    def to_root(src, dst, sem_index, recv, where):
        return pltpu.make_async_remote_copy(
            src_ref=src, dst_ref=dst, send_sem=send_sem.at[sem_index], recv_sem=recv,
            device_id=where, device_id_type=MESH,
        )

    slots = [lax.rem(column - (i * nj + j) + columns, columns) for i, j in root_of]
    load_copies = [
        to_root(l_own, l_all.at[slots[o]], 8 + o, many_sem.at[1], {"ia": root_of[o][0], "ja": root_of[o][1], "ka": o})
        for o in range(nk)
    ]
    slot = jnp.where(ka == 0, slots[0], slots[-1])
    shape_copy = to_root(s_own, s_all.at[slot], 7, many_sem.at[0], {"ia": root_ia, "ja": root_ja})

    @pl.when(ka == 0)
    def _():
        for o, copy in enumerate(load_copies):
            if o:
                copy.start()
            else:
                pl.when(~is_root)(copy.start)

    pl.when(~is_root)(shape_copy.start)

    @pl.when(is_root)
    def _():
        s_all[0] = s_own[...]

        @pl.when(ka == 0)
        def _():
            l_all[0] = l_own[...]

    def halo(src, dst, index, where):
        return pltpu.make_async_remote_copy(
            src_ref=src, dst_ref=dst, send_sem=send_sem.at[index], recv_sem=recv_sem.at[index],
            device_id=where, device_id_type=MESH,
        )

    (has_i0, to_i0), (has_i1, to_i1), (has_j0, to_j0), (has_j1, to_j1) = beside
    has_k0, has_k1 = ka > 0, ka < nk - 1
    copies = [
        (halo(flow.at[li - 2 : li], raw_i.at[0], 0, to_i1), has_i1, has_i0),
        (halo(flow.at[0:2], raw_i.at[1], 1, to_i0), has_i0, has_i1),
        (halo(flow.at[:, :, lj - 2 : lj], raw_j.at[0, :, :, 6:8], 2, to_j1), has_j1, has_j0),
        (halo(flow.at[:, :, 0:2], raw_j.at[1, :, :, 0:2], 3, to_j0), has_j0, has_j1),
        (halo(send_k.at[0], halo_k.at[0], 4, {"ka": jnp.minimum(ka + 1, nk - 1)}), has_k1, has_k0),
        (halo(send_k.at[1], halo_k.at[1], 5, {"ka": jnp.maximum(ka - 1, 0)}), has_k0, has_k1),
    ]
    for copy, sends, _ in copies[0:4]:
        pl.when(sends)(copy.start)

    plane_copies = [
        pltpu.make_async_remote_copy(
            src_ref=planes, dst_ref=planes_in.at[o - 1], send_sem=send_sem.at[15 + o],
            recv_sem=many_sem.at[2], device_id={"ka": lax.rem(ka + o, nk)}, device_id_type=MESH,
        )
        for o in range(1, nk)
    ]
    lane_j = lax.broadcasted_iota(jnp.int32, (lj, 128), 1)
    send_k[...] = jnp.zeros_like(send_k)

    @pl.loop(0, li)
    def _(i):
        here = lane_j // 2 == i
        for c, w in enumerate(primitives([fv[i, c] for c in range(5)])):
            prim[i + 2, c, 8 : 8 + lj] = w
            send_k[0, c] = jnp.where(here, pltpu.roll(w, 2 * i + 2, 1), send_k[0, c])
            send_k[1, c] = jnp.where(here, pltpu.roll(w, 2 * i, 1), send_k[1, c])

    def far(shape, c):
        return jnp.full(shape, FAR_STATE[c], jnp.float32)

    for base, (_, _, gets) in zip((0, li + 2), copies[0:2]):

        @pl.when(~gets)
        def _(base=base):
            for r in range(2):
                for c in range(5):
                    prim[base + r, c, 8 : 8 + lj] = far((lj, lk), c)

    for base, (_, _, gets) in zip((0, 8 + lj), copies[2:4]):

        @pl.when(~gets)
        def _(base=base):
            @pl.loop(0, li)
            def _(i):
                for c in range(5):
                    prim[i + 2, c, base : base + 8] = far((8, lk), c)

    @pl.when(~has_k0)
    def _():
        halo_k[0] = jnp.zeros(halo_k.shape[1:], jnp.float32)

    @pl.when(~has_k1)
    def _():
        for c in range(5):
            halo_k[1, c] = far((lj, 128), c)

    pl.when(~leads)(functools.partial(pl.semaphore_wait, column_sem, 1))
    for copy in plane_copies:
        copy.start()
    for copy, sends, _ in copies[4:6]:
        pl.when(sends)(copy.start)

    pltpu.make_async_copy(planes_in, planes_in, many_sem.at[2]).wait()
    total = planes[...]
    for o in range(nk - 1):
        total = total + planes_in[o]
    wall = mv[...].astype(jnp.float32)
    wall = jnp.concatenate([jnp.zeros((li, 2 * lj), jnp.float32), wall, jnp.zeros((li, 128 - 3 * lj), jnp.float32)], axis=1)
    turned = jnp.concatenate([total + wall, jnp.zeros((128 - li, 128), jnp.float32)], axis=0).T

    for side, (base, (copy, _, gets)) in enumerate(zip((0, 8 + lj), copies[2:4])):

        @pl.when(gets)
        def _(side=side, base=base, copy=copy):
            copy.wait_recv()

            @pl.loop(0, li)
            def _(i):
                for c, w in enumerate(primitives([raw_j[side, i, c] for c in range(5)])):
                    prim[i + 2, c, base : base + 8] = w

    pl.when(has_k0)(copies[4][0].wait_recv)
    pl.when(has_k1)(copies[5][0].wait_recv)

    first = ka * lk
    own_pair = [send_k[0, c] for c in range(5)]
    next_pair = [halo_k[1, c] for c in range(5)]
    last_weight = (1.0 - (first + lk).astype(jnp.float32) / total_k) ** 2
    speed_pairs = jnp.zeros((lj, 128), jnp.float32)
    for i in range(li):
        speed_pairs = jnp.where(lane_j // 2 == i, turned[lj : 2 * lj, i : i + 1], speed_pairs)
    last = faces(
        own_pair,
        [pltpu.roll(w, 127, 1) for w in own_pair],
        next_pair,
        [pltpu.roll(w, 127, 1) for w in next_pair],
        3,
        last_weight * speed_pairs,
    )
    for c in range(5):
        edge_k[c] = last[c]

    def cells(i, lo, rows):
        return [prim[i, c, lo : lo + rows] for c in range(5)]

    def along_i(i):
        return faces(cells(i, 8, lj), cells(i + 1, 8, lj), cells(i + 2, 8, lj), cells(i + 3, 8, lj), 1)

    at_wall = ka == 0
    lane_f = (first + lane_j).astype(jnp.float32)
    face_weight = (1.0 - lane_f / total_k) ** 2
    cell_weight = STRAIN * (1.0 - (lane_f + 0.5) / total_k)
    first_lane, pair_lane, last_lane = lane_j < 1, lane_j < 2, lane_j == lk - 1
    column_lane = lax.broadcasted_iota(jnp.int32, (3 * lj, 128), 1)

    @pl.loop(0, li)
    def _(n):
        i = jnp.where(n < li - 4, n + 2, jnp.where(n < li - 2, n - (li - 4), n))
        for side, (turn, base) in enumerate(((li - 4, 0), (li - 2, li + 2))):

            @pl.when((n == turn) & copies[side][2])
            def _(side=side, base=base):
                copies[side][0].wait_recv()
                for r in range(2):
                    for c, w in enumerate(primitives([raw_i[side, r, c] for c in range(5)])):
                        prim[base + r, c, 8 : 8 + lj] = w

        @pl.when((n == 0) | (n == li - 4) | (n == li - 2))
        def _():
            for c, w in enumerate(along_i(i)):
                flux_i[c] = w

        column_i = jnp.sum(jnp.where(column_lane == i, turned[0 : 3 * lj], 0.0), axis=1, keepdims=True)
        disp_i = column_i[0:lj]
        speed_i = jnp.broadcast_to(column_i[lj : 2 * lj], (lj, 128))
        solid = jnp.broadcast_to(column_i[2 * lj : 3 * lj], (lj, 128)) > 0.5

        upper = along_i(i + 1)
        residual = []
        for c in range(5):
            residual.append(upper[c] - flux_i[c])
            flux_i[c] = upper[c]

        rows = lj + 8
        flux_j = faces(cells(i + 2, 6, rows), cells(i + 2, 7, rows), cells(i + 2, 8, rows), cells(i + 2, 9, rows), 2)
        residual = [r + (f[1 : lj + 1] - f[0:lj]) for r, f in zip(residual, flux_j)]

        below2, below, above = [], [], []
        own = cells(i + 2, 8, lj)
        for c, w in enumerate(own):
            up = jnp.where(last_lane, pltpu.roll(halo_k[1, c], lk - 1 - 2 * i, 1), pltpu.roll(w, lk - 1, 1))
            down = pltpu.roll(w, 1, 1)
            mirror2 = jnp.where(first_lane, up, down)
            mirror1 = w
            if c == 3:
                mirror2 = 2.0 * speed_i - mirror2
                mirror1 = 2.0 * speed_i - mirror1
            mirror2 = jnp.where(solid, mirror2, FAR_STATE[c])
            mirror1 = jnp.where(solid, mirror1, FAR_STATE[c])
            ghost = halo_k[0, c]
            ghost2 = jnp.where(at_wall, mirror2, pltpu.roll(ghost, lax.rem(lk - 2 * i, lk), 1))
            ghost1 = jnp.where(at_wall, mirror1, pltpu.roll(ghost, lk - 1 - 2 * i, 1))
            below2.append(jnp.where(pair_lane, ghost2, pltpu.roll(w, 2, 1)))
            below.append(jnp.where(first_lane, ghost1, down))
            above.append(up)
        flux_k = faces(below2, below, own, above, 3, face_weight * speed_i)
        growth = (-0.5 * SECTION_STEP) * jnp.exp(cell_weight * disp_i)
        for c, f in enumerate(flux_k):
            end = pltpu.roll(edge_k[c], lk - 1 - 2 * i, 1)
            high = jnp.where(last_lane, end, pltpu.roll(f, lk - 1, 1))
            new[i, c] = fv[i, c] + growth * (residual[c] + (high - f))

    for copy, sends, _ in copies:
        pl.when(sends)(copy.wait_send)
    for copy in plane_copies:
        copy.wait_send()
    pl.when(~is_root)(shape_copy.wait_send)

    @pl.when(ka == 0)
    def _():
        for o, copy in enumerate(load_copies):
            if o:
                copy.wait_send()
            else:
                pl.when(~is_root)(copy.wait_send)

    near = min(3, nj)
    line = lax.rem(ia, lines)
    order = sorted(range(lines), key=lambda o: min(o, lines - o))
    direct = [
        {"ia": lax.rem(root_ia + o, lines), "ja": lax.rem(root_ja + j, near)}
        for j in range(near)
        for o in order
        if j or o
    ]
    passed = [
        {"ia": line + lines * h, "ja": j}
        for h in range(ni // lines)
        for j in range(nj)
        if h or j >= near
    ]
    hands_on = (ia < lines) & (ja == jnp.where((line == root_ia) & (root_ja == 0), min(1, nj - 1), 0))

    def give(targets):
        for where in targets:
            pltpu.make_async_remote_copy(
                src_ref=g_own, dst_ref=g_own, send_sem=many_sem.at[4], recv_sem=many_sem.at[3],
                device_id=where, device_id_type=MESH,
            ).start()

    def sent(targets):
        if targets:
            left = l_all.at[0 : len(targets)]
            pltpu.make_async_copy(left, left, many_sem.at[4]).wait()

    @pl.when(is_root)
    def _():
        others = s_all.at[1:columns]
        pltpu.make_async_copy(others, others, many_sem.at[0]).wait()

        @pl.when(ka == 0)
        def _():
            loads = l_all.at[1:columns]
            pltpu.make_async_copy(loads, loads, many_sem.at[1]).wait()

        @pl.when(ka > 0)
        def _():
            pltpu.make_async_copy(l_all, l_all, many_sem.at[1]).wait()

        summed = jnp.sum(s_all[...] * l_all[...], axis=0)
        each = jnp.sum(summed, axis=1, keepdims=True)
        row = lax.broadcasted_iota(jnp.int32, (8, 128), 0)
        g_own[...] = jnp.sum(jnp.where(lane == row, each, 0.0), axis=0, keepdims=True)

        give(direct)
        force[...] = g_own[...]
        sent(direct)

    @pl.when(~is_root)
    def _():
        pltpu.make_async_copy(g_own, g_own, many_sem.at[3]).wait()

        @pl.when(hands_on)
        def _():
            give(passed)

        force[...] = g_own[...]

        @pl.when(hands_on)
        def _():
            sent(passed)


def finish(scale, new, partial, out, force, sem):
    copy = pltpu.make_async_copy(new, out, sem)
    copy.start()
    force[...] = partial[:, 0 : force.shape[1]] * scale
    copy.wait()


def solution(mesh):
    sizes = (mesh.shape["ia"], mesh.shape["ja"], mesh.shape["ka"])
    ni, nj, nk = sizes

    def local(flow_state, mode_shapes, modal_coords, wall_mask):
        li, _, lj, lk = flow_state.shape
        modes = mode_shapes.shape[0]
        f32 = jnp.float32
        tile = pltpu.VMEM((8, 128), f32)
        row = pltpu.VMEM((1, 128), f32)
        vmem = pl.BlockSpec(memory_space=pltpu.VMEM)
        hbm = pl.BlockSpec(memory_space=pltpu.HBM)
        held = functools.partial(pltpu.with_memory_space_constraint, memory_space=pltpu.HBM)
        new, partial = pl.pallas_call(
            functools.partial(section, sizes),
            out_shape=(pltpu.VMEM(flow_state.shape, f32), pltpu.VMEM((1, 128), f32)),
            in_specs=[hbm, hbm, hbm, hbm],
            out_specs=(vmem, vmem),
            scratch_shapes=[
                pltpu.VMEM(flow_state.shape, f32),
                pltpu.VMEM(mode_shapes.shape, f32),
                pltpu.VMEM(wall_mask.shape, jnp.int32),
                pltpu.SMEM(modal_coords.shape, f32),
                pltpu.VMEM((li + 4, 5, lj + 24, lk), f32),
                pltpu.VMEM((2, 2, 5, lj, lk), f32),
                pltpu.VMEM((2, li, 5, 8, lk), f32),
                pltpu.VMEM((2, 5, lj, 128), f32),
                pltpu.VMEM((2, 5, lj, 128), f32),
                pltpu.VMEM((5, lj, 128), f32),
                tile,
                pltpu.VMEM((nk - 1, 8, 128), f32),
                tile,
                row,
                pltpu.VMEM((ni * nj, 8, 128), f32),
                pltpu.VMEM((ni * nj, 1, 128), f32),
                row,
                pltpu.VMEM((5, lj, lk), f32),
                pltpu.SemaphoreType.DMA((4,)),
                pltpu.SemaphoreType.DMA((15 + nk,)),
                pltpu.SemaphoreType.DMA((6,)),
                pltpu.SemaphoreType.DMA((5,)),
                pltpu.SemaphoreType.REGULAR,
            ],
            compiler_params=pltpu.CompilerParams(
                collective_id=0, has_side_effects=True, vmem_limit_bytes=32 * 1024 * 1024
            ),
            name="section",
        )(held(flow_state), held(mode_shapes), held(modal_coords), held(wall_mask))
        out, force = pl.pallas_call(
            functools.partial(finish, 1.0 / math.sqrt(ni * li * nj * lj)),
            out_shape=(
                jax.ShapeDtypeStruct(flow_state.shape, f32),
                jax.ShapeDtypeStruct((1, modes), f32),
            ),
            in_specs=[vmem, vmem],
            out_specs=(hbm, vmem),
            scratch_shapes=[pltpu.SemaphoreType.DMA],
            compiler_params=pltpu.CompilerParams(vmem_limit_bytes=8 * 1024 * 1024),
            name="finish",
        )(new, partial)
        return (out, force.reshape(modes))

    return jax.shard_map(
        local,
        mesh=mesh,
        in_specs=(P("ia", None, "ja", "ka"), P("ka", "ia", "ja"), P(), P("ia", "ja")),
        out_specs=(P("ia", None, "ja", "ka"), P("ka")),
        check_vma=False,
    )
```

```python
import functools
import math

import jax
import jax.numpy as jnp
from jax import lax
from jax.experimental import pallas as pl
from jax.experimental.pallas import tpu as pltpu
from jax.sharding import PartitionSpec as P

MESH = pl.DeviceIdType.MESH
SECTION_STEP = 0.2
STRAIN = 0.25
FAR_PRESSURE = 0.8
ROOT_WALL = (1, 0)
ROOT = (0, 0)
FAR_STATE = (1.0, 0.6, 0.0, 0.0, 0.8)


def primitives(block):
    density, mom_x, mom_y, mom_z, energy = block
    inverse = 1.0 / density
    pressure = 0.4 * (energy - 0.5 * (mom_x * mom_x + mom_y * mom_y + mom_z * mom_z) * inverse)
    return [density, mom_x * inverse, mom_y * inverse, mom_z * inverse, pressure]


def minmod(x, y):
    return jnp.maximum(jnp.minimum(x, jnp.maximum(y, 0.0)), jnp.minimum(y, 0.0))


def side_flux(state, component, grid_speed):
    density, along_x, along_y, along_z, pressure = state
    own = state[component]
    normal = own if grid_speed is None else own - grid_speed
    mom = [density * along_x, density * along_y, density * along_z]
    energy = 2.5 * pressure + 0.5 * (mom[0] * along_x + mom[1] * along_y + mom[2] * along_z)
    conserved = [density] + mom + [energy]
    flux = [quantity * normal for quantity in conserved]
    flux[component] = flux[component] + pressure
    flux[4] = flux[4] + pressure * own
    wave = jnp.abs(normal) + math.sqrt(1.4) * pressure * lax.rsqrt(pressure * density)
    return conserved, flux, wave


def faces(a, b, c, d, component, grid_speed=None):
    left, right = [], []
    for wa, wb, wc, wd in zip(a, b, c, d):
        middle = wc - wb
        left.append(wb + 0.5 * minmod(wb - wa, middle))
        right.append(wc - 0.5 * minmod(middle, wd - wc))
    left_cons, left_flux, left_wave = side_flux(left, component, grid_speed)
    right_cons, right_flux, right_wave = side_flux(right, component, grid_speed)
    wave = jnp.maximum(left_wave, right_wave)
    return [
        lf + rf - wave * (rc - lc)
        for lf, rf, lc, rc in zip(left_flux, right_flux, left_cons, right_cons)
    ]


def section(
    sizes, flow, shapes, coords_in, mask, new, force,
    fv, sv, mv, coords, prim, raw_i, raw_j, send_k, halo_k, edge_k, planes, planes_in,
    s_own, l_own, s_all, l_all, g_own, flux_i,
    local_sem, send_sem, recv_sem, many_sem, column_sem,
):
    ni, nj, nk = sizes
    ia, ja, ka = lax.axis_index("ia"), lax.axis_index("ja"), lax.axis_index("ka")
    li, lj, lk = flow.shape[0], flow.shape[2], flow.shape[3]
    modes = shapes.shape[0]
    columns = ni * nj
    lines = 8 if ni % 8 == 0 else ni
    root_of = [(i % lines, j % nj) for i, j in [ROOT_WALL] + [ROOT] * (nk - 1)]
    root_ia = jnp.where(ka == 0, root_of[0][0], root_of[-1][0])
    root_ja = jnp.where(ka == 0, root_of[0][1], root_of[-1][1])
    column = ia * nj + ja
    is_root = column == root_ia * nj + root_ja
    total_k = nk * lk

    in_flow = pltpu.make_async_copy(flow, fv, local_sem.at[0])
    in_shapes = pltpu.make_async_copy(shapes, sv, local_sem.at[1])
    in_mask = pltpu.make_async_copy(mask, mv, local_sem.at[2])
    in_coords = pltpu.make_async_copy(coords_in, coords, local_sem.at[3])
    in_flow.start()
    in_shapes.start()
    in_mask.start()
    in_coords.start()

    barrier = pltpu.get_barrier_semaphore()

    def greet(where):
        pl.semaphore_signal(barrier, inc=1, device_id=where, device_id_type=MESH)

    @pl.when(is_root)
    def _():
        def next_to(c):
            c = lax.rem(2 * columns - c + column, columns)
            return {"ia": c // nj, "ja": lax.rem(c, nj)}

        @pl.when(ka > 0)
        def _():
            @pl.loop(0, columns)
            def _(c):
                greet({**next_to(c), "ka": 0})

        @pl.loop(1, columns)
        def _(c):
            greet(next_to(c))

    beside = [
        (ia > 0, {"ia": jnp.maximum(ia - 1, 0)}),
        (ia < ni - 1, {"ia": jnp.minimum(ia + 1, ni - 1)}),
        (ja > 0, {"ja": jnp.maximum(ja - 1, 0)}),
        (ja < nj - 1, {"ja": jnp.minimum(ja + 1, nj - 1)}),
    ]
    expected = jnp.where(is_root, 0, 1) + jnp.where(ka == 0, nk - 1, 0)
    for there, where in beside:
        pl.when(there)(functools.partial(greet, where))
        expected = expected + there.astype(jnp.int32)
    lead = nk // 2
    leads = ka == lead
    pl.when(~leads)(functools.partial(greet, {"ka": lead}))
    expected = expected + jnp.where(leads, nk - 1, 0)

    lane = lax.broadcasted_iota(jnp.int32, (8, 128), 1)

    in_shapes.wait()
    in_mask.wait()
    in_coords.wait()
    packed = jnp.zeros((modes, 128), jnp.float32)
    disp = jnp.zeros((li, lj), jnp.float32)
    speed = jnp.zeros((li, lj), jnp.float32)
    zeros = jnp.zeros((modes, 128 - lj), jnp.float32)
    for i in range(li):
        wide = jnp.concatenate([sv[:, i, :], zeros], axis=1)
        packed = packed + (pltpu.roll(wide, lj * i, 1) if i else wide)
    for m in range(modes):
        one = sv[m]
        disp = disp + coords[0, ka * modes + m] * one
        speed = speed + coords[1, ka * modes + m] * one
    s_own[...] = packed
    planes[...] = jnp.concatenate([disp, speed, jnp.zeros((li, 128 - 2 * lj), jnp.float32)], axis=1)

    in_flow.wait()

    @pl.when(ka == 0)
    def _():
        lane_t = lax.broadcasted_iota(jnp.int32, (lj, 128), 1)
        turned = jnp.zeros((lj, 128), jnp.float32)
        for i in range(li):
            p = primitives([fv[i, c, :, 0:1] for c in range(5)])[4]
            turned = turned + jnp.where(lax.rem(lane_t, li) == i, p - FAR_PRESSURE, 0.0)
        flat = jnp.concatenate([turned] * (128 // lj), axis=0).T[0:li]
        keep = jnp.concatenate([mv[...]] * (128 // lj), axis=1)
        own_row = lane // lj == lax.broadcasted_iota(jnp.int32, (8, 128), 0)
        l_own[...] = jnp.sum(jnp.where(own_row & (keep == 1), flat, 0.0), axis=0, keepdims=True)

    pl.semaphore_wait(barrier, expected)

    @pl.when(leads)
    def _():
        for o in range(1, nk):
            pl.semaphore_signal(
                column_sem, inc=1, device_id={"ka": lax.rem(ka + o, nk)}, device_id_type=MESH
            )

    def to_root(src, dst, sem_index, recv, where):
        return pltpu.make_async_remote_copy(
            src_ref=src, dst_ref=dst, send_sem=send_sem.at[sem_index], recv_sem=recv,
            device_id=where, device_id_type=MESH,
        )

    slots = [lax.rem(column - (i * nj + j) + columns, columns) for i, j in root_of]
    load_copies = [
        to_root(l_own, l_all.at[slots[o]], 8 + o, many_sem.at[1], {"ia": root_of[o][0], "ja": root_of[o][1], "ka": o})
        for o in range(nk)
    ]
    slot = jnp.where(ka == 0, slots[0], slots[-1])
    shape_copy = to_root(s_own, s_all.at[slot], 7, many_sem.at[0], {"ia": root_ia, "ja": root_ja})

    @pl.when(ka == 0)
    def _():
        for o, copy in enumerate(load_copies):
            if o:
                copy.start()
            else:
                pl.when(~is_root)(copy.start)

    pl.when(~is_root)(shape_copy.start)

    @pl.when(is_root)
    def _():
        s_all[0] = s_own[...]

        @pl.when(ka == 0)
        def _():
            l_all[0] = l_own[...]

    def halo(src, dst, index, where):
        return pltpu.make_async_remote_copy(
            src_ref=src, dst_ref=dst, send_sem=send_sem.at[index], recv_sem=recv_sem.at[index],
            device_id=where, device_id_type=MESH,
        )

    (has_i0, to_i0), (has_i1, to_i1), (has_j0, to_j0), (has_j1, to_j1) = beside
    has_k0, has_k1 = ka > 0, ka < nk - 1
    copies = [
        (halo(flow.at[li - 2 : li], raw_i.at[0], 0, to_i1), has_i1, has_i0),
        (halo(flow.at[0:2], raw_i.at[1], 1, to_i0), has_i0, has_i1),
        (halo(flow.at[:, :, lj - 2 : lj], raw_j.at[0, :, :, 6:8], 2, to_j1), has_j1, has_j0),
        (halo(flow.at[:, :, 0:2], raw_j.at[1, :, :, 0:2], 3, to_j0), has_j0, has_j1),
        (halo(send_k.at[0], halo_k.at[0], 4, {"ka": jnp.minimum(ka + 1, nk - 1)}), has_k1, has_k0),
        (halo(send_k.at[1], halo_k.at[1], 5, {"ka": jnp.maximum(ka - 1, 0)}), has_k0, has_k1),
    ]
    for copy, sends, _ in copies[0:4]:
        pl.when(sends)(copy.start)

    plane_copies = [
        pltpu.make_async_remote_copy(
            src_ref=planes, dst_ref=planes_in.at[o - 1], send_sem=send_sem.at[15 + o],
            recv_sem=many_sem.at[2], device_id={"ka": lax.rem(ka + o, nk)}, device_id_type=MESH,
        )
        for o in range(1, nk)
    ]
    lane_j = lax.broadcasted_iota(jnp.int32, (lj, 128), 1)
    send_k[...] = jnp.zeros_like(send_k)

    @pl.loop(0, li)
    def _(i):
        here = lane_j // 2 == i
        for c, w in enumerate(primitives([fv[i, c] for c in range(5)])):
            prim[i + 2, c, 8 : 8 + lj] = w
            send_k[0, c] = jnp.where(here, pltpu.roll(w, 2 * i + 2, 1), send_k[0, c])
            send_k[1, c] = jnp.where(here, pltpu.roll(w, 2 * i, 1), send_k[1, c])

    def far(shape, c):
        return jnp.full(shape, FAR_STATE[c], jnp.float32)

    for base, (_, _, gets) in zip((0, li + 2), copies[0:2]):

        @pl.when(~gets)
        def _(base=base):
            for r in range(2):
                for c in range(5):
                    prim[base + r, c, 8 : 8 + lj] = far((lj, lk), c)

    for base, (_, _, gets) in zip((0, 8 + lj), copies[2:4]):

        @pl.when(~gets)
        def _(base=base):
            @pl.loop(0, li)
            def _(i):
                for c in range(5):
                    prim[i + 2, c, base : base + 8] = far((8, lk), c)

    @pl.when(~has_k0)
    def _():
        halo_k[0] = jnp.zeros(halo_k.shape[1:], jnp.float32)

    @pl.when(~has_k1)
    def _():
        for c in range(5):
            halo_k[1, c] = far((lj, 128), c)

    pl.when(~leads)(functools.partial(pl.semaphore_wait, column_sem, 1))
    for copy in plane_copies:
        copy.start()
    for copy, sends, _ in copies[4:6]:
        pl.when(sends)(copy.start)

    pltpu.make_async_copy(planes_in, planes_in, many_sem.at[2]).wait()
    total = planes[...]
    for o in range(nk - 1):
        total = total + planes_in[o]
    wall = mv[...].astype(jnp.float32)
    wall = jnp.concatenate([jnp.zeros((li, 2 * lj), jnp.float32), wall, jnp.zeros((li, 128 - 3 * lj), jnp.float32)], axis=1)
    turned = jnp.concatenate([total + wall, jnp.zeros((128 - li, 128), jnp.float32)], axis=0).T

    for side, (base, (copy, _, gets)) in enumerate(zip((0, 8 + lj), copies[2:4])):

        @pl.when(gets)
        def _(side=side, base=base, copy=copy):
            copy.wait_recv()

            @pl.loop(0, li)
            def _(i):
                for c, w in enumerate(primitives([raw_j[side, i, c] for c in range(5)])):
                    prim[i + 2, c, base : base + 8] = w

    pl.when(has_k0)(copies[4][0].wait_recv)
    pl.when(has_k1)(copies[5][0].wait_recv)

    first = ka * lk
    own_pair = [send_k[0, c] for c in range(5)]
    next_pair = [halo_k[1, c] for c in range(5)]
    last_weight = (1.0 - (first + lk).astype(jnp.float32) / total_k) ** 2
    speed_pairs = jnp.zeros((lj, 128), jnp.float32)
    for i in range(li):
        speed_pairs = jnp.where(lane_j // 2 == i, turned[lj : 2 * lj, i : i + 1], speed_pairs)
    last = faces(
        own_pair,
        [pltpu.roll(w, 127, 1) for w in own_pair],
        next_pair,
        [pltpu.roll(w, 127, 1) for w in next_pair],
        3,
        last_weight * speed_pairs,
    )
    for c in range(5):
        edge_k[c] = last[c]

    def cells(i, lo, rows):
        return [prim[i, c, lo : lo + rows] for c in range(5)]

    def along_i(i):
        return faces(cells(i, 8, lj), cells(i + 1, 8, lj), cells(i + 2, 8, lj), cells(i + 3, 8, lj), 1)

    at_wall = ka == 0
    lane_f = (first + lane_j).astype(jnp.float32)
    face_weight = (1.0 - lane_f / total_k) ** 2
    cell_weight = STRAIN * (1.0 - (lane_f + 0.5) / total_k)
    first_lane, pair_lane, last_lane = lane_j < 1, lane_j < 2, lane_j == lk - 1
    column_lane = lax.broadcasted_iota(jnp.int32, (3 * lj, 128), 1)

    @pl.loop(0, li)
    def _(n):
        i = jnp.where(n < li - 4, n + 2, jnp.where(n < li - 2, n - (li - 4), n))
        for side, (turn, base) in enumerate(((li - 4, 0), (li - 2, li + 2))):

            @pl.when((n == turn) & copies[side][2])
            def _(side=side, base=base):
                copies[side][0].wait_recv()
                for r in range(2):
                    for c, w in enumerate(primitives([raw_i[side, r, c] for c in range(5)])):
                        prim[base + r, c, 8 : 8 + lj] = w

        @pl.when((n == 0) | (n == li - 4) | (n == li - 2))
        def _():
            for c, w in enumerate(along_i(i)):
                flux_i[c] = w

        column_i = jnp.sum(jnp.where(column_lane == i, turned[0 : 3 * lj], 0.0), axis=1, keepdims=True)
        disp_i = column_i[0:lj]
        speed_i = jnp.broadcast_to(column_i[lj : 2 * lj], (lj, 128))
        solid = jnp.broadcast_to(column_i[2 * lj : 3 * lj], (lj, 128)) > 0.5

        upper = along_i(i + 1)
        residual = []
        for c in range(5):
            residual.append(upper[c] - flux_i[c])
            flux_i[c] = upper[c]

        rows = lj + 8
        flux_j = faces(cells(i + 2, 6, rows), cells(i + 2, 7, rows), cells(i + 2, 8, rows), cells(i + 2, 9, rows), 2)
        residual = [r + (f[1 : lj + 1] - f[0:lj]) for r, f in zip(residual, flux_j)]

        below2, below, above = [], [], []
        own = cells(i + 2, 8, lj)
        for c, w in enumerate(own):
            up = jnp.where(last_lane, pltpu.roll(halo_k[1, c], lk - 1 - 2 * i, 1), pltpu.roll(w, lk - 1, 1))
            down = pltpu.roll(w, 1, 1)
            mirror2 = jnp.where(first_lane, up, down)
            mirror1 = w
            if c == 3:
                mirror2 = 2.0 * speed_i - mirror2
                mirror1 = 2.0 * speed_i - mirror1
            mirror2 = jnp.where(solid, mirror2, FAR_STATE[c])
            mirror1 = jnp.where(solid, mirror1, FAR_STATE[c])
            ghost = halo_k[0, c]
            ghost2 = jnp.where(at_wall, mirror2, pltpu.roll(ghost, lax.rem(lk - 2 * i, lk), 1))
            ghost1 = jnp.where(at_wall, mirror1, pltpu.roll(ghost, lk - 1 - 2 * i, 1))
            below2.append(jnp.where(pair_lane, ghost2, pltpu.roll(w, 2, 1)))
            below.append(jnp.where(first_lane, ghost1, down))
            above.append(up)
        flux_k = faces(below2, below, own, above, 3, face_weight * speed_i)
        growth = (-0.5 * SECTION_STEP) * jnp.exp(cell_weight * disp_i)
        for c, f in enumerate(flux_k):
            end = pltpu.roll(edge_k[c], lk - 1 - 2 * i, 1)
            high = jnp.where(last_lane, end, pltpu.roll(f, lk - 1, 1))
            new[i, c] = fv[i, c] + growth * (residual[c] + (high - f))

    for copy, sends, _ in copies:
        pl.when(sends)(copy.wait_send)
    for copy in plane_copies:
        copy.wait_send()
    pl.when(~is_root)(shape_copy.wait_send)

    @pl.when(ka == 0)
    def _():
        for o, copy in enumerate(load_copies):
            if o:
                copy.wait_send()
            else:
                pl.when(~is_root)(copy.wait_send)

    near = min(4, nj)
    line = lax.rem(ia, lines)
    order = [o % lines for o in (1, 4, 5, 2, 3, 6, 7, 0)][:lines] if lines == 8 else list(range(lines))
    direct = [
        {"ia": lax.rem(root_ia + o, lines), "ja": lax.rem(root_ja + j, near)}
        for j in range(near)
        for o in order
        if j or o
    ]
    passed = [
        {"ia": line + lines * h, "ja": j}
        for h in range(ni // lines)
        for j in range(nj)
        if h or j >= near
    ]
    hands_on = (ia < lines) & (ja == near - 1)

    def give(targets):
        for where in targets:
            pltpu.make_async_remote_copy(
                src_ref=g_own, dst_ref=g_own, send_sem=many_sem.at[4], recv_sem=many_sem.at[3],
                device_id=where, device_id_type=MESH,
            ).start()

    def sent(targets):
        if targets:
            left = l_all.at[0 : len(targets)]
            pltpu.make_async_copy(left, left, many_sem.at[4]).wait()

    @pl.when(is_root)
    def _():
        others = s_all.at[1:columns]
        pltpu.make_async_copy(others, others, many_sem.at[0]).wait()

        @pl.when(ka == 0)
        def _():
            loads = l_all.at[1:columns]
            pltpu.make_async_copy(loads, loads, many_sem.at[1]).wait()

        @pl.when(ka > 0)
        def _():
            pltpu.make_async_copy(l_all, l_all, many_sem.at[1]).wait()

        summed = jnp.sum(s_all[...] * l_all[...], axis=0)
        each = jnp.sum(summed, axis=1, keepdims=True)
        row = lax.broadcasted_iota(jnp.int32, (8, 128), 0)
        g_own[...] = jnp.sum(jnp.where(lane == row, each, 0.0), axis=0, keepdims=True)

        give(direct)
        force[...] = g_own[...]
        sent(direct)

    @pl.when(~is_root)
    def _():
        pltpu.make_async_copy(g_own, g_own, many_sem.at[3]).wait()

        @pl.when(hands_on)
        def _():
            give(passed)

        force[...] = g_own[...]

        @pl.when(hands_on)
        def _():
            sent(passed)


def finish(scale, new, partial, out, force, sem):
    copy = pltpu.make_async_copy(new, out, sem)
    copy.start()
    force[...] = partial[:, 0 : force.shape[1]] * scale
    copy.wait()


def solution(mesh):
    sizes = (mesh.shape["ia"], mesh.shape["ja"], mesh.shape["ka"])
    ni, nj, nk = sizes

    def local(flow_state, mode_shapes, modal_coords, wall_mask):
        li, _, lj, lk = flow_state.shape
        modes = mode_shapes.shape[0]
        f32 = jnp.float32
        tile = pltpu.VMEM((8, 128), f32)
        row = pltpu.VMEM((1, 128), f32)
        vmem = pl.BlockSpec(memory_space=pltpu.VMEM)
        hbm = pl.BlockSpec(memory_space=pltpu.HBM)
        held = functools.partial(pltpu.with_memory_space_constraint, memory_space=pltpu.HBM)
        new, partial = pl.pallas_call(
            functools.partial(section, sizes),
            out_shape=(pltpu.VMEM(flow_state.shape, f32), pltpu.VMEM((1, 128), f32)),
            in_specs=[hbm, hbm, hbm, hbm],
            out_specs=(vmem, vmem),
            scratch_shapes=[
                pltpu.VMEM(flow_state.shape, f32),
                pltpu.VMEM(mode_shapes.shape, f32),
                pltpu.VMEM(wall_mask.shape, jnp.int32),
                pltpu.SMEM(modal_coords.shape, f32),
                pltpu.VMEM((li + 4, 5, lj + 24, lk), f32),
                pltpu.VMEM((2, 2, 5, lj, lk), f32),
                pltpu.VMEM((2, li, 5, 8, lk), f32),
                pltpu.VMEM((2, 5, lj, 128), f32),
                pltpu.VMEM((2, 5, lj, 128), f32),
                pltpu.VMEM((5, lj, 128), f32),
                tile,
                pltpu.VMEM((nk - 1, 8, 128), f32),
                tile,
                row,
                pltpu.VMEM((ni * nj, 8, 128), f32),
                pltpu.VMEM((ni * nj, 1, 128), f32),
                row,
                pltpu.VMEM((5, lj, lk), f32),
                pltpu.SemaphoreType.DMA((4,)),
                pltpu.SemaphoreType.DMA((15 + nk,)),
                pltpu.SemaphoreType.DMA((6,)),
                pltpu.SemaphoreType.DMA((5,)),
                pltpu.SemaphoreType.REGULAR,
            ],
            compiler_params=pltpu.CompilerParams(
                collective_id=0, has_side_effects=True, vmem_limit_bytes=32 * 1024 * 1024
            ),
            name="section",
        )(held(flow_state), held(mode_shapes), held(modal_coords), held(wall_mask))
        out, force = pl.pallas_call(
            functools.partial(finish, 1.0 / math.sqrt(ni * li * nj * lj)),
            out_shape=(
                jax.ShapeDtypeStruct(flow_state.shape, f32),
                jax.ShapeDtypeStruct((1, modes), f32),
            ),
            in_specs=[vmem, vmem],
            out_specs=(hbm, vmem),
            scratch_shapes=[pltpu.SemaphoreType.DMA],
            compiler_params=pltpu.CompilerParams(vmem_limit_bytes=8 * 1024 * 1024),
            name="finish",
        )(new, partial)
        return (out, force.reshape(modes))

    return jax.shard_map(
        local,
        mesh=mesh,
        in_specs=(P("ia", None, "ja", "ka"), P("ka", "ia", "ja"), P(), P("ia", "ja")),
        out_specs=(P("ia", None, "ja", "ka"), P("ka")),
        check_vma=False,
    )
```

```python
import functools
import math

import jax
import jax.numpy as jnp
from jax import lax
from jax.experimental import pallas as pl
from jax.experimental.pallas import tpu as pltpu
from jax.sharding import PartitionSpec as P

MESH = pl.DeviceIdType.MESH
SECTION_STEP = 0.2
STRAIN = 0.25
FAR_PRESSURE = 0.8
FAR_STATE = (1.0, 0.6, 0.0, 0.0, 0.8)


def primitives(block):
    density, mom_x, mom_y, mom_z, energy = block
    inverse = 1.0 / density
    pressure = 0.4 * (energy - 0.5 * (mom_x * mom_x + mom_y * mom_y + mom_z * mom_z) * inverse)
    return [density, mom_x * inverse, mom_y * inverse, mom_z * inverse, pressure]


def minmod(x, y):
    return jnp.maximum(jnp.minimum(x, jnp.maximum(y, 0.0)), jnp.minimum(y, 0.0))


def side_flux(state, component, grid_speed):
    density, along_x, along_y, along_z, pressure = state
    own = state[component]
    normal = own if grid_speed is None else own - grid_speed
    mom = [density * along_x, density * along_y, density * along_z]
    energy = 2.5 * pressure + 0.5 * (mom[0] * along_x + mom[1] * along_y + mom[2] * along_z)
    conserved = [density] + mom + [energy]
    flux = [quantity * normal for quantity in conserved]
    flux[component] = flux[component] + pressure
    flux[4] = flux[4] + pressure * own
    wave = jnp.abs(normal) + math.sqrt(1.4) * pressure * lax.rsqrt(pressure * density)
    return conserved, flux, wave


def faces(a, b, c, d, component, grid_speed=None):
    left, right = [], []
    for wa, wb, wc, wd in zip(a, b, c, d):
        middle = wc - wb
        left.append(wb + 0.5 * minmod(wb - wa, middle))
        right.append(wc - 0.5 * minmod(middle, wd - wc))
    left_cons, left_flux, left_wave = side_flux(left, component, grid_speed)
    right_cons, right_flux, right_wave = side_flux(right, component, grid_speed)
    wave = jnp.maximum(left_wave, right_wave)
    return [
        lf + rf - wave * (rc - lc)
        for lf, rf, lc, rc in zip(left_flux, right_flux, left_cons, right_cons)
    ]


def section(
    sizes, flow, shapes, coords_in, mask, new, force,
    fv, sv, mv, coords, prim, raw_i, raw_j, send_k, halo_k, edge_k, planes, planes_in,
    s_own, l_own, s_all, l_all, g_sum, g_own, flux_i,
    local_sem, send_sem, recv_sem, many_sem, column_sem,
):
    ni, nj, nk = sizes
    ia, ja, ka = lax.axis_index("ia"), lax.axis_index("ja"), lax.axis_index("ka")
    li, lj, lk = flow.shape[0], flow.shape[2], flow.shape[3]
    modes = shapes.shape[0]
    columns = ni * nj
    lines = 8 if ni % 8 == 0 else ni
    root_of = [(1 - o % 2, o + 1 - o % 2) for o in range(nk)]
    odd = lax.rem(ka, 2) == 1
    root_ia = jnp.where(odd, 0, 1)
    root_ka = jnp.where(odd, ka, ka + 1 - lax.rem(ka, 2))
    column = ia * nj + ja
    own_root = odd & (column == 0)
    other_root = odd & (column == nj)
    is_root = own_root | other_root
    serves = jnp.where(own_root, ka, jnp.maximum(ka - 1, 0))
    total_k = nk * lk

    in_flow = pltpu.make_async_copy(flow, fv, local_sem.at[0])
    in_shapes = pltpu.make_async_copy(shapes, sv, local_sem.at[1])
    in_mask = pltpu.make_async_copy(mask, mv, local_sem.at[2])
    in_coords = pltpu.make_async_copy(coords_in, coords, local_sem.at[3])
    in_flow.start()
    in_shapes.start()
    in_mask.start()
    in_coords.start()

    barrier = pltpu.get_barrier_semaphore()

    def greet(where):
        pl.semaphore_signal(barrier, inc=1, device_id=where, device_id_type=MESH)

    @pl.when(is_root)
    def _():
        def next_to(c):
            c = lax.rem(2 * columns - c + column, columns)
            return {"ia": c // nj, "ja": lax.rem(c, nj)}

        @pl.loop(0, columns)
        def _(c):
            greet({**next_to(c), "ka": 0})

        @pl.when(serves > 0)
        def _():
            @pl.loop(1, columns)
            def _(c):
                greet({**next_to(c), "ka": serves})

            pl.when(other_root)(functools.partial(greet, {"ka": serves}))

    beside = [
        (ia > 0, {"ia": jnp.maximum(ia - 1, 0)}),
        (ia < ni - 1, {"ia": jnp.minimum(ia + 1, ni - 1)}),
        (ja > 0, {"ja": jnp.maximum(ja - 1, 0)}),
        (ja < nj - 1, {"ja": jnp.minimum(ja + 1, nj - 1)}),
    ]
    expected = jnp.where(own_root, 0, 1) + jnp.where(ka == 0, nk - 1, 0)
    for there, where in beside:
        pl.when(there)(functools.partial(greet, where))
        expected = expected + there.astype(jnp.int32)
    lead = nk // 2
    leads = ka == lead
    pl.when(~leads)(functools.partial(greet, {"ka": lead}))
    expected = expected + jnp.where(leads, nk - 1, 0)

    lane = lax.broadcasted_iota(jnp.int32, (8, 128), 1)

    in_shapes.wait()
    in_mask.wait()
    in_coords.wait()
    packed = jnp.zeros((modes, 128), jnp.float32)
    disp = jnp.zeros((li, lj), jnp.float32)
    speed = jnp.zeros((li, lj), jnp.float32)
    zeros = jnp.zeros((modes, 128 - lj), jnp.float32)
    for i in range(li):
        wide = jnp.concatenate([sv[:, i, :], zeros], axis=1)
        packed = packed + (pltpu.roll(wide, lj * i, 1) if i else wide)
    for m in range(modes):
        one = sv[m]
        disp = disp + coords[0, ka * modes + m] * one
        speed = speed + coords[1, ka * modes + m] * one
    s_own[...] = packed
    planes[...] = jnp.concatenate([disp, speed, jnp.zeros((li, 128 - 2 * lj), jnp.float32)], axis=1)

    in_flow.wait()

    @pl.when(ka == 0)
    def _():
        lane_t = lax.broadcasted_iota(jnp.int32, (lj, 128), 1)
        turned = jnp.zeros((lj, 128), jnp.float32)
        for i in range(li):
            p = primitives([fv[i, c, :, 0:1] for c in range(5)])[4]
            turned = turned + jnp.where(lax.rem(lane_t, li) == i, p - FAR_PRESSURE, 0.0)
        flat = jnp.concatenate([turned] * (128 // lj), axis=0).T[0:li]
        keep = jnp.concatenate([mv[...]] * (128 // lj), axis=1)
        own_row = lane // lj == lax.broadcasted_iota(jnp.int32, (8, 128), 0)
        l_own[...] = jnp.sum(jnp.where(own_row & (keep == 1), flat, 0.0), axis=0, keepdims=True)

    pl.semaphore_wait(barrier, expected)

    @pl.when(leads)
    def _():
        for o in range(1, nk):
            pl.semaphore_signal(
                column_sem, inc=1, device_id={"ka": lax.rem(ka + o, nk)}, device_id_type=MESH
            )

    def to_root(src, dst, sem_index, recv, where):
        return pltpu.make_async_remote_copy(
            src_ref=src, dst_ref=dst, send_sem=send_sem.at[sem_index], recv_sem=recv,
            device_id=where, device_id_type=MESH,
        )

    slots = [lax.rem(column - i * nj + columns, columns) for i, _ in root_of]
    load_copies = [
        to_root(l_own, l_all.at[slots[o]], 8 + o, many_sem.at[1], {"ia": root_of[o][0], "ja": 0, "ka": root_of[o][1]})
        for o in range(nk)
    ]
    slot = jnp.where(odd, slots[1], slots[0])
    shape_copy = to_root(s_own, s_all.at[slot], 7, many_sem.at[0], {"ia": root_ia, "ja": 0, "ka": root_ka})

    @pl.when(ka == 0)
    def _():
        for copy in load_copies:
            copy.start()

    pl.when(~own_root)(shape_copy.start)

    @pl.when(own_root)
    def _():
        s_all[0] = s_own[...]

    def halo(src, dst, index, where):
        return pltpu.make_async_remote_copy(
            src_ref=src, dst_ref=dst, send_sem=send_sem.at[index], recv_sem=recv_sem.at[index],
            device_id=where, device_id_type=MESH,
        )

    (has_i0, to_i0), (has_i1, to_i1), (has_j0, to_j0), (has_j1, to_j1) = beside
    has_k0, has_k1 = ka > 0, ka < nk - 1
    copies = [
        (halo(flow.at[li - 2 : li], raw_i.at[0], 0, to_i1), has_i1, has_i0),
        (halo(flow.at[0:2], raw_i.at[1], 1, to_i0), has_i0, has_i1),
        (halo(flow.at[:, :, lj - 2 : lj], raw_j.at[0, :, :, 6:8], 2, to_j1), has_j1, has_j0),
        (halo(flow.at[:, :, 0:2], raw_j.at[1, :, :, 0:2], 3, to_j0), has_j0, has_j1),
        (halo(send_k.at[0], halo_k.at[0], 4, {"ka": jnp.minimum(ka + 1, nk - 1)}), has_k1, has_k0),
        (halo(send_k.at[1], halo_k.at[1], 5, {"ka": jnp.maximum(ka - 1, 0)}), has_k0, has_k1),
    ]
    for copy, sends, _ in copies[0:4]:
        pl.when(sends)(copy.start)

    plane_copies = [
        pltpu.make_async_remote_copy(
            src_ref=planes, dst_ref=planes_in.at[o - 1], send_sem=send_sem.at[15 + o],
            recv_sem=many_sem.at[2], device_id={"ka": lax.rem(ka + o, nk)}, device_id_type=MESH,
        )
        for o in range(1, nk)
    ]
    lane_j = lax.broadcasted_iota(jnp.int32, (lj, 128), 1)
    send_k[...] = jnp.zeros_like(send_k)

    @pl.loop(0, li)
    def _(i):
        here = lane_j // 2 == i
        for c, w in enumerate(primitives([fv[i, c] for c in range(5)])):
            prim[i + 2, c, 8 : 8 + lj] = w
            send_k[0, c] = jnp.where(here, pltpu.roll(w, 2 * i + 2, 1), send_k[0, c])
            send_k[1, c] = jnp.where(here, pltpu.roll(w, 2 * i, 1), send_k[1, c])

    def far(shape, c):
        return jnp.full(shape, FAR_STATE[c], jnp.float32)

    for base, (_, _, gets) in zip((0, li + 2), copies[0:2]):

        @pl.when(~gets)
        def _(base=base):
            for r in range(2):
                for c in range(5):
                    prim[base + r, c, 8 : 8 + lj] = far((lj, lk), c)

    for base, (_, _, gets) in zip((0, 8 + lj), copies[2:4]):

        @pl.when(~gets)
        def _(base=base):
            @pl.loop(0, li)
            def _(i):
                for c in range(5):
                    prim[i + 2, c, base : base + 8] = far((8, lk), c)

    @pl.when(~has_k0)
    def _():
        halo_k[0] = jnp.zeros(halo_k.shape[1:], jnp.float32)

    @pl.when(~has_k1)
    def _():
        for c in range(5):
            halo_k[1, c] = far((lj, 128), c)

    pl.when(~leads)(functools.partial(pl.semaphore_wait, column_sem, 1))
    for copy in plane_copies:
        copy.start()
    for copy, sends, _ in copies[4:6]:
        pl.when(sends)(copy.start)

    pltpu.make_async_copy(planes_in, planes_in, many_sem.at[2]).wait()
    total = planes[...]
    for o in range(nk - 1):
        total = total + planes_in[o]
    wall = mv[...].astype(jnp.float32)
    wall = jnp.concatenate([jnp.zeros((li, 2 * lj), jnp.float32), wall, jnp.zeros((li, 128 - 3 * lj), jnp.float32)], axis=1)
    turned = jnp.concatenate([total + wall, jnp.zeros((128 - li, 128), jnp.float32)], axis=0).T

    for side, (base, (copy, _, gets)) in enumerate(zip((0, 8 + lj), copies[2:4])):

        @pl.when(gets)
        def _(side=side, base=base, copy=copy):
            copy.wait_recv()

            @pl.loop(0, li)
            def _(i):
                for c, w in enumerate(primitives([raw_j[side, i, c] for c in range(5)])):
                    prim[i + 2, c, base : base + 8] = w

    pl.when(has_k0)(copies[4][0].wait_recv)
    pl.when(has_k1)(copies[5][0].wait_recv)

    first = ka * lk
    own_pair = [send_k[0, c] for c in range(5)]
    next_pair = [halo_k[1, c] for c in range(5)]
    last_weight = (1.0 - (first + lk).astype(jnp.float32) / total_k) ** 2
    speed_pairs = jnp.zeros((lj, 128), jnp.float32)
    for i in range(li):
        speed_pairs = jnp.where(lane_j // 2 == i, turned[lj : 2 * lj, i : i + 1], speed_pairs)
    last = faces(
        own_pair,
        [pltpu.roll(w, 127, 1) for w in own_pair],
        next_pair,
        [pltpu.roll(w, 127, 1) for w in next_pair],
        3,
        last_weight * speed_pairs,
    )
    for c in range(5):
        edge_k[c] = last[c]

    def cells(i, lo, rows):
        return [prim[i, c, lo : lo + rows] for c in range(5)]

    def along_i(i):
        return faces(cells(i, 8, lj), cells(i + 1, 8, lj), cells(i + 2, 8, lj), cells(i + 3, 8, lj), 1)

    at_wall = ka == 0
    lane_f = (first + lane_j).astype(jnp.float32)
    face_weight = (1.0 - lane_f / total_k) ** 2
    cell_weight = STRAIN * (1.0 - (lane_f + 0.5) / total_k)
    first_lane, pair_lane, last_lane = lane_j < 1, lane_j < 2, lane_j == lk - 1
    column_lane = lax.broadcasted_iota(jnp.int32, (3 * lj, 128), 1)

    @pl.loop(0, li)
    def _(n):
        i = jnp.where(n < li - 4, n + 2, jnp.where(n < li - 2, n - (li - 4), n))
        for side, (turn, base) in enumerate(((li - 4, 0), (li - 2, li + 2))):

            @pl.when((n == turn) & copies[side][2])
            def _(side=side, base=base):
                copies[side][0].wait_recv()
                for r in range(2):
                    for c, w in enumerate(primitives([raw_i[side, r, c] for c in range(5)])):
                        prim[base + r, c, 8 : 8 + lj] = w

        @pl.when((n == 0) | (n == li - 4) | (n == li - 2))
        def _():
            for c, w in enumerate(along_i(i)):
                flux_i[c] = w

        column_i = jnp.sum(jnp.where(column_lane == i, turned[0 : 3 * lj], 0.0), axis=1, keepdims=True)
        disp_i = column_i[0:lj]
        speed_i = jnp.broadcast_to(column_i[lj : 2 * lj], (lj, 128))
        solid = jnp.broadcast_to(column_i[2 * lj : 3 * lj], (lj, 128)) > 0.5

        upper = along_i(i + 1)
        residual = []
        for c in range(5):
            residual.append(upper[c] - flux_i[c])
            flux_i[c] = upper[c]

        rows = lj + 8
        flux_j = faces(cells(i + 2, 6, rows), cells(i + 2, 7, rows), cells(i + 2, 8, rows), cells(i + 2, 9, rows), 2)
        residual = [r + (f[1 : lj + 1] - f[0:lj]) for r, f in zip(residual, flux_j)]

        below2, below, above = [], [], []
        own = cells(i + 2, 8, lj)
        for c, w in enumerate(own):
            up = jnp.where(last_lane, pltpu.roll(halo_k[1, c], lk - 1 - 2 * i, 1), pltpu.roll(w, lk - 1, 1))
            down = pltpu.roll(w, 1, 1)
            mirror2 = jnp.where(first_lane, up, down)
            mirror1 = w
            if c == 3:
                mirror2 = 2.0 * speed_i - mirror2
                mirror1 = 2.0 * speed_i - mirror1
            mirror2 = jnp.where(solid, mirror2, FAR_STATE[c])
            mirror1 = jnp.where(solid, mirror1, FAR_STATE[c])
            ghost = halo_k[0, c]
            ghost2 = jnp.where(at_wall, mirror2, pltpu.roll(ghost, lax.rem(lk - 2 * i, lk), 1))
            ghost1 = jnp.where(at_wall, mirror1, pltpu.roll(ghost, lk - 1 - 2 * i, 1))
            below2.append(jnp.where(pair_lane, ghost2, pltpu.roll(w, 2, 1)))
            below.append(jnp.where(first_lane, ghost1, down))
            above.append(up)
        flux_k = faces(below2, below, own, above, 3, face_weight * speed_i)
        growth = (-0.5 * SECTION_STEP) * jnp.exp(cell_weight * disp_i)
        for c, f in enumerate(flux_k):
            end = pltpu.roll(edge_k[c], lk - 1 - 2 * i, 1)
            high = jnp.where(last_lane, end, pltpu.roll(f, lk - 1, 1))
            new[i, c] = fv[i, c] + growth * (residual[c] + (high - f))

    for copy, sends, _ in copies:
        pl.when(sends)(copy.wait_send)
    for copy in plane_copies:
        copy.wait_send()
    pl.when(~own_root)(shape_copy.wait_send)

    @pl.when(ka == 0)
    def _():
        for copy in load_copies:
            copy.wait_send()

    near = min(4, nj)
    line = lax.rem(ia, lines)
    order = [o % lines for o in (7, 4, 6, 5, 1, 3, 2, 0)][:lines] if lines == 8 else list(range(lines))
    direct = [
        {"ia": lax.rem(ia + o, lines), "ja": j, "ka": serves}
        for j in range(near)
        for o in order
        if j or o
    ]
    passed = [
        {"ia": line + lines * h, "ja": j}
        for h in range(ni // lines)
        for j in range(nj)
        if h or j >= near
    ]
    hands_on = (ia < lines) & (ja == near - 1)

    def give(source, targets):
        for where in targets:
            pltpu.make_async_remote_copy(
                src_ref=source, dst_ref=g_own, send_sem=many_sem.at[4], recv_sem=many_sem.at[3],
                device_id=where, device_id_type=MESH,
            ).start()

    def sent(targets):
        if targets:
            left = l_all.at[0 : len(targets)]
            pltpu.make_async_copy(left, left, many_sem.at[4]).wait()

    @pl.when(is_root)
    def _():
        @pl.when(own_root)
        def _():
            others = s_all.at[1:columns]
            pltpu.make_async_copy(others, others, many_sem.at[0]).wait()

        @pl.when(other_root)
        def _():
            pltpu.make_async_copy(s_all, s_all, many_sem.at[0]).wait()

        pltpu.make_async_copy(l_all, l_all, many_sem.at[1]).wait()
        summed = jnp.sum(s_all[...] * l_all[...], axis=0)
        each = jnp.sum(summed, axis=1, keepdims=True)
        row = lax.broadcasted_iota(jnp.int32, (8, 128), 0)
        g_sum[...] = jnp.sum(jnp.where(lane == row, each, 0.0), axis=0, keepdims=True)
        give(g_sum, direct)
        beside_core = [{"ka": serves}]

        @pl.when(other_root)
        def _():
            give(g_sum, beside_core)
            sent(direct + beside_core)

        @pl.when(own_root)
        def _():
            force[...] = g_sum[...]
            sent(direct)

    @pl.when(~own_root)
    def _():
        pltpu.make_async_copy(g_own, g_own, many_sem.at[3]).wait()
        pl.when(hands_on)(functools.partial(give, g_own, passed))
        force[...] = g_own[...]
        pl.when(hands_on)(functools.partial(sent, passed))


def finish(scale, new, partial, out, force, sem):
    copy = pltpu.make_async_copy(new, out, sem)
    copy.start()
    force[...] = partial[:, 0 : force.shape[1]] * scale
    copy.wait()


def solution(mesh):
    sizes = (mesh.shape["ia"], mesh.shape["ja"], mesh.shape["ka"])
    ni, nj, nk = sizes

    def local(flow_state, mode_shapes, modal_coords, wall_mask):
        li, _, lj, lk = flow_state.shape
        modes = mode_shapes.shape[0]
        f32 = jnp.float32
        tile = pltpu.VMEM((8, 128), f32)
        row = pltpu.VMEM((1, 128), f32)
        vmem = pl.BlockSpec(memory_space=pltpu.VMEM)
        hbm = pl.BlockSpec(memory_space=pltpu.HBM)
        held = functools.partial(pltpu.with_memory_space_constraint, memory_space=pltpu.HBM)
        new, partial = pl.pallas_call(
            functools.partial(section, sizes),
            out_shape=(pltpu.VMEM(flow_state.shape, f32), pltpu.VMEM((1, 128), f32)),
            in_specs=[hbm, hbm, hbm, hbm],
            out_specs=(vmem, vmem),
            scratch_shapes=[
                pltpu.VMEM(flow_state.shape, f32),
                pltpu.VMEM(mode_shapes.shape, f32),
                pltpu.VMEM(wall_mask.shape, jnp.int32),
                pltpu.SMEM(modal_coords.shape, f32),
                pltpu.VMEM((li + 4, 5, lj + 24, lk), f32),
                pltpu.VMEM((2, 2, 5, lj, lk), f32),
                pltpu.VMEM((2, li, 5, 8, lk), f32),
                pltpu.VMEM((2, 5, lj, 128), f32),
                pltpu.VMEM((2, 5, lj, 128), f32),
                pltpu.VMEM((5, lj, 128), f32),
                tile,
                pltpu.VMEM((nk - 1, 8, 128), f32),
                tile,
                row,
                pltpu.VMEM((ni * nj, 8, 128), f32),
                pltpu.VMEM((ni * nj, 1, 128), f32),
                row,
                row,
                pltpu.VMEM((5, lj, lk), f32),
                pltpu.SemaphoreType.DMA((4,)),
                pltpu.SemaphoreType.DMA((15 + nk,)),
                pltpu.SemaphoreType.DMA((6,)),
                pltpu.SemaphoreType.DMA((5,)),
                pltpu.SemaphoreType.REGULAR,
            ],
            compiler_params=pltpu.CompilerParams(
                collective_id=0, has_side_effects=True, vmem_limit_bytes=32 * 1024 * 1024
            ),
            name="section",
        )(held(flow_state), held(mode_shapes), held(modal_coords), held(wall_mask))
        out, force = pl.pallas_call(
            functools.partial(finish, 1.0 / math.sqrt(ni * li * nj * lj)),
            out_shape=(
                jax.ShapeDtypeStruct(flow_state.shape, f32),
                jax.ShapeDtypeStruct((1, modes), f32),
            ),
            in_specs=[vmem, vmem],
            out_specs=(hbm, vmem),
            scratch_shapes=[pltpu.SemaphoreType.DMA],
            compiler_params=pltpu.CompilerParams(vmem_limit_bytes=8 * 1024 * 1024),
            name="finish",
        )(new, partial)
        return (out, force.reshape(modes))

    return jax.shard_map(
        local,
        mesh=mesh,
        in_specs=(P("ia", None, "ja", "ka"), P("ka", "ia", "ja"), P(), P("ia", "ja")),
        out_specs=(P("ia", None, "ja", "ka"), P("ka")),
        check_vma=False,
    )
```

```python
import functools
import math

import jax
import jax.numpy as jnp
from jax import lax
from jax.experimental import pallas as pl
from jax.experimental.pallas import tpu as pltpu
from jax.sharding import PartitionSpec as P

MESH = pl.DeviceIdType.MESH
SECTION_STEP = 0.2
STRAIN = 0.25
FAR_PRESSURE = 0.8
FAR_STATE = (1.0, 0.6, 0.0, 0.0, 0.8)


def primitives(block):
    density, mom_x, mom_y, mom_z, energy = block
    inverse = 1.0 / density
    pressure = 0.4 * (energy - 0.5 * (mom_x * mom_x + mom_y * mom_y + mom_z * mom_z) * inverse)
    return [density, mom_x * inverse, mom_y * inverse, mom_z * inverse, pressure]


def minmod(x, y):
    return jnp.maximum(jnp.minimum(x, jnp.maximum(y, 0.0)), jnp.minimum(y, 0.0))


def side_flux(state, component, grid_speed):
    density, along_x, along_y, along_z, pressure = state
    own = state[component]
    normal = own if grid_speed is None else own - grid_speed
    mom = [density * along_x, density * along_y, density * along_z]
    energy = 2.5 * pressure + 0.5 * (mom[0] * along_x + mom[1] * along_y + mom[2] * along_z)
    conserved = [density] + mom + [energy]
    flux = [quantity * normal for quantity in conserved]
    flux[component] = flux[component] + pressure
    flux[4] = flux[4] + pressure * own
    wave = jnp.abs(normal) + math.sqrt(1.4) * pressure * lax.rsqrt(pressure * density)
    return conserved, flux, wave


def faces(a, b, c, d, component, grid_speed=None):
    left, right = [], []
    for wa, wb, wc, wd in zip(a, b, c, d):
        middle = wc - wb
        left.append(wb + 0.5 * minmod(wb - wa, middle))
        right.append(wc - 0.5 * minmod(middle, wd - wc))
    left_cons, left_flux, left_wave = side_flux(left, component, grid_speed)
    right_cons, right_flux, right_wave = side_flux(right, component, grid_speed)
    wave = jnp.maximum(left_wave, right_wave)
    return [
        lf + rf - wave * (rc - lc)
        for lf, rf, lc, rc in zip(left_flux, right_flux, left_cons, right_cons)
    ]


def section(
    sizes, flow, shapes, coords_in, mask, new, force,
    fv, sv, mv, coords, prim, raw_i, raw_j, send_k, halo_k, edge_k, planes, planes_in,
    s_own, l_own, s_all, l_all, g_sum, g_own, flux_i,
    local_sem, send_sem, recv_sem, many_sem, column_sem, edge_sem,
):
    ni, nj, nk = sizes
    ia, ja, ka = lax.axis_index("ia"), lax.axis_index("ja"), lax.axis_index("ka")
    li, lj, lk = flow.shape[0], flow.shape[2], flow.shape[3]
    modes = shapes.shape[0]
    columns = ni * nj
    lines = 8 if ni % 8 == 0 else ni
    root_of = [(1 - o % 2, o + 1 - o % 2) for o in range(nk)]
    odd = lax.rem(ka, 2) == 1
    root_ia = jnp.where(odd, 0, 1)
    root_ka = jnp.where(odd, ka, ka + 1 - lax.rem(ka, 2))
    column = ia * nj + ja
    own_root = odd & (column == 0)
    other_root = odd & (column == nj)
    is_root = own_root | other_root
    serves = jnp.where(own_root, ka, jnp.maximum(ka - 1, 0))
    total_k = nk * lk

    in_flow = pltpu.make_async_copy(flow, fv, local_sem.at[0])
    in_shapes = pltpu.make_async_copy(shapes, sv, local_sem.at[1])
    in_mask = pltpu.make_async_copy(mask, mv, local_sem.at[2])
    in_coords = pltpu.make_async_copy(coords_in, coords, local_sem.at[3])
    in_flow.start()
    in_shapes.start()
    in_mask.start()
    in_coords.start()

    barrier = pltpu.get_barrier_semaphore()

    def greet(where):
        pl.semaphore_signal(barrier, inc=1, device_id=where, device_id_type=MESH)

    @pl.when(is_root)
    def _():
        def next_to(c):
            c = lax.rem(2 * columns - c + column, columns)
            return {"ia": c // nj, "ja": lax.rem(c, nj)}

        @pl.loop(0, columns)
        def _(c):
            greet({**next_to(c), "ka": 0})

        @pl.when(serves > 0)
        def _():
            @pl.loop(1, columns)
            def _(c):
                greet({**next_to(c), "ka": serves})

            pl.when(other_root)(functools.partial(greet, {"ka": serves}))

    beside = [
        (ia > 0, {"ia": jnp.maximum(ia - 1, 0)}),
        (ia < ni - 1, {"ia": jnp.minimum(ia + 1, ni - 1)}),
        (ja > 0, {"ja": jnp.maximum(ja - 1, 0)}),
        (ja < nj - 1, {"ja": jnp.minimum(ja + 1, nj - 1)}),
    ]
    expected = jnp.where(own_root, 0, 1) + jnp.where(ka == 0, nk - 1, 0)
    for (below, _), (above, where) in (beside[0:2], beside[2:4]):
        pl.when(above)(functools.partial(greet, where))
        expected = expected + below.astype(jnp.int32)
    lead = nk // 2
    leads = ka == lead
    pl.when(~leads)(functools.partial(greet, {"ka": lead}))
    expected = expected + jnp.where(leads, nk - 1, 0)

    lane = lax.broadcasted_iota(jnp.int32, (8, 128), 1)

    in_shapes.wait()
    in_mask.wait()
    in_coords.wait()
    packed = jnp.zeros((modes, 128), jnp.float32)
    disp = jnp.zeros((li, lj), jnp.float32)
    speed = jnp.zeros((li, lj), jnp.float32)
    zeros = jnp.zeros((modes, 128 - lj), jnp.float32)
    for i in range(li):
        wide = jnp.concatenate([sv[:, i, :], zeros], axis=1)
        packed = packed + (pltpu.roll(wide, lj * i, 1) if i else wide)
    for m in range(modes):
        one = sv[m]
        disp = disp + coords[0, ka * modes + m] * one
        speed = speed + coords[1, ka * modes + m] * one
    s_own[...] = packed
    planes[...] = jnp.concatenate([disp, speed, jnp.zeros((li, 128 - 2 * lj), jnp.float32)], axis=1)

    in_flow.wait()

    @pl.when(ka == 0)
    def _():
        lane_t = lax.broadcasted_iota(jnp.int32, (lj, 128), 1)
        turned = jnp.zeros((lj, 128), jnp.float32)
        for i in range(li):
            p = primitives([fv[i, c, :, 0:1] for c in range(5)])[4]
            turned = turned + jnp.where(lax.rem(lane_t, li) == i, p - FAR_PRESSURE, 0.0)
        flat = jnp.concatenate([turned] * (128 // lj), axis=0).T[0:li]
        keep = jnp.concatenate([mv[...]] * (128 // lj), axis=1)
        own_row = lane // lj == lax.broadcasted_iota(jnp.int32, (8, 128), 0)
        l_own[...] = jnp.sum(jnp.where(own_row & (keep == 1), flat, 0.0), axis=0, keepdims=True)

    pl.when(expected > 0)(functools.partial(pl.semaphore_wait, barrier, expected))
    for axis, (there, where) in enumerate((beside[0], beside[2])):

        @pl.when(there)
        def _(axis=axis, where=where):
            pl.semaphore_signal(edge_sem.at[axis], inc=1, device_id=where, device_id_type=MESH)

    @pl.when(leads)
    def _():
        for o in range(1, nk):
            pl.semaphore_signal(
                column_sem, inc=1, device_id={"ka": lax.rem(ka + o, nk)}, device_id_type=MESH
            )

    def to_root(src, dst, sem_index, recv, where):
        return pltpu.make_async_remote_copy(
            src_ref=src, dst_ref=dst, send_sem=send_sem.at[sem_index], recv_sem=recv,
            device_id=where, device_id_type=MESH,
        )

    slots = [lax.rem(column - i * nj + columns, columns) for i, _ in root_of]
    load_copies = [
        to_root(l_own, l_all.at[slots[o]], 8 + o, many_sem.at[1], {"ia": root_of[o][0], "ja": 0, "ka": root_of[o][1]})
        for o in range(nk)
    ]
    slot = jnp.where(odd, slots[1], slots[0])
    shape_copy = to_root(s_own, s_all.at[slot], 7, many_sem.at[0], {"ia": root_ia, "ja": 0, "ka": root_ka})

    @pl.when(ka == 0)
    def _():
        for copy in load_copies:
            copy.start()

    pl.when(~own_root)(shape_copy.start)

    @pl.when(own_root)
    def _():
        s_all[0] = s_own[...]

    def halo(src, dst, index, where):
        return pltpu.make_async_remote_copy(
            src_ref=src, dst_ref=dst, send_sem=send_sem.at[index], recv_sem=recv_sem.at[index],
            device_id=where, device_id_type=MESH,
        )

    (has_i0, to_i0), (has_i1, to_i1), (has_j0, to_j0), (has_j1, to_j1) = beside
    has_k0, has_k1 = ka > 0, ka < nk - 1
    copies = [
        (halo(flow.at[li - 2 : li], raw_i.at[0], 0, to_i1), has_i1, has_i0),
        (halo(flow.at[0:2], raw_i.at[1], 1, to_i0), has_i0, has_i1),
        (halo(flow.at[:, :, lj - 2 : lj], raw_j.at[0, :, :, 6:8], 2, to_j1), has_j1, has_j0),
        (halo(flow.at[:, :, 0:2], raw_j.at[1, :, :, 0:2], 3, to_j0), has_j0, has_j1),
        (halo(send_k.at[0], halo_k.at[0], 4, {"ka": jnp.minimum(ka + 1, nk - 1)}), has_k1, has_k0),
        (halo(send_k.at[1], halo_k.at[1], 5, {"ka": jnp.maximum(ka - 1, 0)}), has_k0, has_k1),
    ]
    for copy, sends, _ in (copies[1], copies[3]):
        pl.when(sends)(copy.start)

    plane_copies = [
        pltpu.make_async_remote_copy(
            src_ref=planes, dst_ref=planes_in.at[o - 1], send_sem=send_sem.at[15 + o],
            recv_sem=many_sem.at[2], device_id={"ka": lax.rem(ka + o, nk)}, device_id_type=MESH,
        )
        for o in range(1, nk)
    ]
    lane_j = lax.broadcasted_iota(jnp.int32, (lj, 128), 1)
    send_k[...] = jnp.zeros_like(send_k)

    @pl.loop(0, li)
    def _(i):
        here = lane_j // 2 == i
        for c, w in enumerate(primitives([fv[i, c] for c in range(5)])):
            prim[i + 2, c, 8 : 8 + lj] = w
            send_k[0, c] = jnp.where(here, pltpu.roll(w, 2 * i + 2, 1), send_k[0, c])
            send_k[1, c] = jnp.where(here, pltpu.roll(w, 2 * i, 1), send_k[1, c])

    def far(shape, c):
        return jnp.full(shape, FAR_STATE[c], jnp.float32)

    for base, (_, _, gets) in zip((0, li + 2), copies[0:2]):

        @pl.when(~gets)
        def _(base=base):
            for r in range(2):
                for c in range(5):
                    prim[base + r, c, 8 : 8 + lj] = far((lj, lk), c)

    for base, (_, _, gets) in zip((0, 8 + lj), copies[2:4]):

        @pl.when(~gets)
        def _(base=base):
            @pl.loop(0, li)
            def _(i):
                for c in range(5):
                    prim[i + 2, c, base : base + 8] = far((8, lk), c)

    @pl.when(~has_k0)
    def _():
        halo_k[0] = jnp.zeros(halo_k.shape[1:], jnp.float32)

    @pl.when(~has_k1)
    def _():
        for c in range(5):
            halo_k[1, c] = far((lj, 128), c)

    pl.when(~leads)(functools.partial(pl.semaphore_wait, column_sem, 1))
    for copy in plane_copies:
        copy.start()
    for copy, sends, _ in copies[4:6]:
        pl.when(sends)(copy.start)
    for axis, (copy, sends, _) in ((1, copies[2]), (0, copies[0])):

        @pl.when(sends)
        def _(axis=axis, copy=copy):
            pl.semaphore_wait(edge_sem.at[axis], 1)
            copy.start()

    pltpu.make_async_copy(planes_in, planes_in, many_sem.at[2]).wait()
    total = planes[...]
    for o in range(nk - 1):
        total = total + planes_in[o]
    wall = mv[...].astype(jnp.float32)
    wall = jnp.concatenate([jnp.zeros((li, 2 * lj), jnp.float32), wall, jnp.zeros((li, 128 - 3 * lj), jnp.float32)], axis=1)
    turned = jnp.concatenate([total + wall, jnp.zeros((128 - li, 128), jnp.float32)], axis=0).T

    for side, (base, (copy, _, gets)) in enumerate(zip((0, 8 + lj), copies[2:4])):

        @pl.when(gets)
        def _(side=side, base=base, copy=copy):
            copy.wait_recv()

            @pl.loop(0, li)
            def _(i):
                for c, w in enumerate(primitives([raw_j[side, i, c] for c in range(5)])):
                    prim[i + 2, c, base : base + 8] = w

    pl.when(has_k0)(copies[4][0].wait_recv)
    pl.when(has_k1)(copies[5][0].wait_recv)

    first = ka * lk
    own_pair = [send_k[0, c] for c in range(5)]
    next_pair = [halo_k[1, c] for c in range(5)]
    last_weight = (1.0 - (first + lk).astype(jnp.float32) / total_k) ** 2
    speed_pairs = jnp.zeros((lj, 128), jnp.float32)
    for i in range(li):
        speed_pairs = jnp.where(lane_j // 2 == i, turned[lj : 2 * lj, i : i + 1], speed_pairs)
    last = faces(
        own_pair,
        [pltpu.roll(w, 127, 1) for w in own_pair],
        next_pair,
        [pltpu.roll(w, 127, 1) for w in next_pair],
        3,
        last_weight * speed_pairs,
    )
    for c in range(5):
        edge_k[c] = last[c]

    def cells(i, lo, rows):
        return [prim[i, c, lo : lo + rows] for c in range(5)]

    def along_i(i):
        return faces(cells(i, 8, lj), cells(i + 1, 8, lj), cells(i + 2, 8, lj), cells(i + 3, 8, lj), 1)

    at_wall = ka == 0
    lane_f = (first + lane_j).astype(jnp.float32)
    face_weight = (1.0 - lane_f / total_k) ** 2
    cell_weight = STRAIN * (1.0 - (lane_f + 0.5) / total_k)
    first_lane, pair_lane, last_lane = lane_j < 1, lane_j < 2, lane_j == lk - 1
    column_lane = lax.broadcasted_iota(jnp.int32, (3 * lj, 128), 1)

    @pl.loop(0, li)
    def _(n):
        i = jnp.where(n < li - 4, n + 2, jnp.where(n < li - 2, n - (li - 4), n))
        for side, (turn, base) in enumerate(((li - 4, 0), (li - 2, li + 2))):

            @pl.when((n == turn) & copies[side][2])
            def _(side=side, base=base):
                copies[side][0].wait_recv()
                for r in range(2):
                    for c, w in enumerate(primitives([raw_i[side, r, c] for c in range(5)])):
                        prim[base + r, c, 8 : 8 + lj] = w

        @pl.when((n == 0) | (n == li - 4) | (n == li - 2))
        def _():
            for c, w in enumerate(along_i(i)):
                flux_i[c] = w

        column_i = jnp.sum(jnp.where(column_lane == i, turned[0 : 3 * lj], 0.0), axis=1, keepdims=True)
        disp_i = column_i[0:lj]
        speed_i = jnp.broadcast_to(column_i[lj : 2 * lj], (lj, 128))
        solid = jnp.broadcast_to(column_i[2 * lj : 3 * lj], (lj, 128)) > 0.5

        upper = along_i(i + 1)
        residual = []
        for c in range(5):
            residual.append(upper[c] - flux_i[c])
            flux_i[c] = upper[c]

        rows = lj + 8
        flux_j = faces(cells(i + 2, 6, rows), cells(i + 2, 7, rows), cells(i + 2, 8, rows), cells(i + 2, 9, rows), 2)
        residual = [r + (f[1 : lj + 1] - f[0:lj]) for r, f in zip(residual, flux_j)]

        below2, below, above = [], [], []
        own = cells(i + 2, 8, lj)
        for c, w in enumerate(own):
            up = jnp.where(last_lane, pltpu.roll(halo_k[1, c], lk - 1 - 2 * i, 1), pltpu.roll(w, lk - 1, 1))
            down = pltpu.roll(w, 1, 1)
            mirror2 = jnp.where(first_lane, up, down)
            mirror1 = w
            if c == 3:
                mirror2 = 2.0 * speed_i - mirror2
                mirror1 = 2.0 * speed_i - mirror1
            mirror2 = jnp.where(solid, mirror2, FAR_STATE[c])
            mirror1 = jnp.where(solid, mirror1, FAR_STATE[c])
            ghost = halo_k[0, c]
            ghost2 = jnp.where(at_wall, mirror2, pltpu.roll(ghost, lax.rem(lk - 2 * i, lk), 1))
            ghost1 = jnp.where(at_wall, mirror1, pltpu.roll(ghost, lk - 1 - 2 * i, 1))
            below2.append(jnp.where(pair_lane, ghost2, pltpu.roll(w, 2, 1)))
            below.append(jnp.where(first_lane, ghost1, down))
            above.append(up)
        flux_k = faces(below2, below, own, above, 3, face_weight * speed_i)
        growth = (-0.5 * SECTION_STEP) * jnp.exp(cell_weight * disp_i)
        for c, f in enumerate(flux_k):
            end = pltpu.roll(edge_k[c], lk - 1 - 2 * i, 1)
            high = jnp.where(last_lane, end, pltpu.roll(f, lk - 1, 1))
            new[i, c] = fv[i, c] + growth * (residual[c] + (high - f))

    for copy, sends, _ in copies:
        pl.when(sends)(copy.wait_send)
    for copy in plane_copies:
        copy.wait_send()
    pl.when(~own_root)(shape_copy.wait_send)

    @pl.when(ka == 0)
    def _():
        for copy in load_copies:
            copy.wait_send()

    near = min(4, nj)
    line = lax.rem(ia, lines)
    order = [o % lines for o in (7, 4, 6, 5, 1, 3, 2, 0)][:lines] if lines == 8 else list(range(lines))
    direct = [
        {"ia": lax.rem(ia + o, lines), "ja": j, "ka": serves}
        for j in range(near)
        for o in order
        if j or o
    ]
    passed = [
        {"ia": line + lines * h, "ja": j}
        for h in range(ni // lines)
        for j in range(nj)
        if h or j >= near
    ]
    hands_on = (ia < lines) & (ja == near - 1)

    def give(source, targets):
        for where in targets:
            pltpu.make_async_remote_copy(
                src_ref=source, dst_ref=g_own, send_sem=many_sem.at[4], recv_sem=many_sem.at[3],
                device_id=where, device_id_type=MESH,
            ).start()

    def sent(targets):
        if targets:
            left = l_all.at[0 : len(targets)]
            pltpu.make_async_copy(left, left, many_sem.at[4]).wait()

    @pl.when(is_root)
    def _():
        @pl.when(own_root)
        def _():
            others = s_all.at[1:columns]
            pltpu.make_async_copy(others, others, many_sem.at[0]).wait()

        @pl.when(other_root)
        def _():
            pltpu.make_async_copy(s_all, s_all, many_sem.at[0]).wait()

        pltpu.make_async_copy(l_all, l_all, many_sem.at[1]).wait()
        summed = jnp.sum(s_all[...] * l_all[...], axis=0)
        each = jnp.sum(summed, axis=1, keepdims=True)
        row = lax.broadcasted_iota(jnp.int32, (8, 128), 0)
        g_sum[...] = jnp.sum(jnp.where(lane == row, each, 0.0), axis=0, keepdims=True)
        give(g_sum, direct)
        beside_core = [{"ka": serves}]

        @pl.when(other_root)
        def _():
            give(g_sum, beside_core)
            sent(direct + beside_core)

        @pl.when(own_root)
        def _():
            force[...] = g_sum[...]
            sent(direct)

    @pl.when(~own_root)
    def _():
        pltpu.make_async_copy(g_own, g_own, many_sem.at[3]).wait()
        pl.when(hands_on)(functools.partial(give, g_own, passed))
        force[...] = g_own[...]
        pl.when(hands_on)(functools.partial(sent, passed))


def finish(scale, new, partial, out, force, sem):
    copy = pltpu.make_async_copy(new, out, sem)
    copy.start()
    force[...] = partial[:, 0 : force.shape[1]] * scale
    copy.wait()


def solution(mesh):
    sizes = (mesh.shape["ia"], mesh.shape["ja"], mesh.shape["ka"])
    ni, nj, nk = sizes

    def local(flow_state, mode_shapes, modal_coords, wall_mask):
        li, _, lj, lk = flow_state.shape
        modes = mode_shapes.shape[0]
        f32 = jnp.float32
        tile = pltpu.VMEM((8, 128), f32)
        row = pltpu.VMEM((1, 128), f32)
        vmem = pl.BlockSpec(memory_space=pltpu.VMEM)
        hbm = pl.BlockSpec(memory_space=pltpu.HBM)
        held = functools.partial(pltpu.with_memory_space_constraint, memory_space=pltpu.HBM)
        new, partial = pl.pallas_call(
            functools.partial(section, sizes),
            out_shape=(pltpu.VMEM(flow_state.shape, f32), pltpu.VMEM((1, 128), f32)),
            in_specs=[hbm, hbm, hbm, hbm],
            out_specs=(vmem, vmem),
            scratch_shapes=[
                pltpu.VMEM(flow_state.shape, f32),
                pltpu.VMEM(mode_shapes.shape, f32),
                pltpu.VMEM(wall_mask.shape, jnp.int32),
                pltpu.SMEM(modal_coords.shape, f32),
                pltpu.VMEM((li + 4, 5, lj + 24, lk), f32),
                pltpu.VMEM((2, 2, 5, lj, lk), f32),
                pltpu.VMEM((2, li, 5, 8, lk), f32),
                pltpu.VMEM((2, 5, lj, 128), f32),
                pltpu.VMEM((2, 5, lj, 128), f32),
                pltpu.VMEM((5, lj, 128), f32),
                tile,
                pltpu.VMEM((nk - 1, 8, 128), f32),
                tile,
                row,
                pltpu.VMEM((ni * nj, 8, 128), f32),
                pltpu.VMEM((ni * nj, 1, 128), f32),
                row,
                row,
                pltpu.VMEM((5, lj, lk), f32),
                pltpu.SemaphoreType.DMA((4,)),
                pltpu.SemaphoreType.DMA((15 + nk,)),
                pltpu.SemaphoreType.DMA((6,)),
                pltpu.SemaphoreType.DMA((5,)),
                pltpu.SemaphoreType.REGULAR,
                pltpu.SemaphoreType.REGULAR((2,)),
            ],
            compiler_params=pltpu.CompilerParams(
                collective_id=0, has_side_effects=True, vmem_limit_bytes=32 * 1024 * 1024
            ),
            name="section",
        )(held(flow_state), held(mode_shapes), held(modal_coords), held(wall_mask))
        out, force = pl.pallas_call(
            functools.partial(finish, 1.0 / math.sqrt(ni * li * nj * lj)),
            out_shape=(
                jax.ShapeDtypeStruct(flow_state.shape, f32),
                jax.ShapeDtypeStruct((1, modes), f32),
            ),
            in_specs=[vmem, vmem],
            out_specs=(hbm, vmem),
            scratch_shapes=[pltpu.SemaphoreType.DMA],
            compiler_params=pltpu.CompilerParams(vmem_limit_bytes=8 * 1024 * 1024),
            name="finish",
        )(new, partial)
        return (out, force.reshape(modes))

    return jax.shard_map(
        local,
        mesh=mesh,
        in_specs=(P("ia", None, "ja", "ka"), P("ka", "ia", "ja"), P(), P("ia", "ja")),
        out_specs=(P("ia", None, "ja", "ka"), P("ka")),
        check_vma=False,
    )
```

```python
import functools
import math

import jax
import jax.numpy as jnp
from jax import lax
from jax.experimental import pallas as pl
from jax.experimental.pallas import tpu as pltpu
from jax.sharding import PartitionSpec as P

MESH = pl.DeviceIdType.MESH
SECTION_STEP = 0.2
STRAIN = 0.25
FAR_PRESSURE = 0.8
FAR_STATE = (1.0, 0.6, 0.0, 0.0, 0.8)


def primitives(block):
    density, mom_x, mom_y, mom_z, energy = block
    inverse = 1.0 / density
    pressure = 0.4 * (energy - 0.5 * (mom_x * mom_x + mom_y * mom_y + mom_z * mom_z) * inverse)
    return [density, mom_x * inverse, mom_y * inverse, mom_z * inverse, pressure]


def minmod(x, y):
    return jnp.maximum(jnp.minimum(x, jnp.maximum(y, 0.0)), jnp.minimum(y, 0.0))


def side_flux(state, component, grid_speed):
    density, along_x, along_y, along_z, pressure = state
    own = state[component]
    normal = own if grid_speed is None else own - grid_speed
    mom = [density * along_x, density * along_y, density * along_z]
    energy = 2.5 * pressure + 0.5 * (mom[0] * along_x + mom[1] * along_y + mom[2] * along_z)
    conserved = [density] + mom + [energy]
    flux = [quantity * normal for quantity in conserved]
    flux[component] = flux[component] + pressure
    flux[4] = flux[4] + pressure * own
    wave = jnp.abs(normal) + math.sqrt(1.4) * pressure * lax.rsqrt(pressure * density)
    return conserved, flux, wave


def faces(a, b, c, d, component, grid_speed=None):
    left, right = [], []
    for wa, wb, wc, wd in zip(a, b, c, d):
        middle = wc - wb
        left.append(wb + 0.5 * minmod(wb - wa, middle))
        right.append(wc - 0.5 * minmod(middle, wd - wc))
    left_cons, left_flux, left_wave = side_flux(left, component, grid_speed)
    right_cons, right_flux, right_wave = side_flux(right, component, grid_speed)
    wave = jnp.maximum(left_wave, right_wave)
    return [
        lf + rf - wave * (rc - lc)
        for lf, rf, lc, rc in zip(left_flux, right_flux, left_cons, right_cons)
    ]


def section(
    sizes, flow, shapes, coords_in, mask, new, force,
    fv, sv, mv, coords, prim, raw_i, raw_j, send_k, halo_k, edge_k, planes, planes_in,
    s_own, l_own, s_all, l_all, g_sum, g_own, flux_i,
    local_sem, send_sem, recv_sem, many_sem, column_sem, edge_sem,
):
    ni, nj, nk = sizes
    ia, ja, ka = lax.axis_index("ia"), lax.axis_index("ja"), lax.axis_index("ka")
    li, lj, lk = flow.shape[0], flow.shape[2], flow.shape[3]
    modes = shapes.shape[0]
    columns = ni * nj
    lines = 8 if ni % 8 == 0 else ni
    root_of = [(1 - o % 2, o + 1 - o % 2) for o in range(nk)]
    odd = lax.rem(ka, 2) == 1
    root_ia = jnp.where(odd, 0, 1)
    root_ka = jnp.where(odd, ka, ka + 1 - lax.rem(ka, 2))
    column = ia * nj + ja
    own_root = odd & (column == 0)
    other_root = odd & (column == nj)
    is_root = own_root | other_root
    serves = jnp.where(own_root, ka, jnp.maximum(ka - 1, 0))
    total_k = nk * lk

    in_flow = pltpu.make_async_copy(flow, fv, local_sem.at[0])
    in_shapes = pltpu.make_async_copy(shapes, sv, local_sem.at[1])
    in_mask = pltpu.make_async_copy(mask, mv, local_sem.at[2])
    in_coords = pltpu.make_async_copy(coords_in, coords, local_sem.at[3])
    in_flow.start()
    in_shapes.start()
    in_mask.start()
    in_coords.start()

    barrier = pltpu.get_barrier_semaphore()

    def greet(where):
        pl.semaphore_signal(barrier, inc=1, device_id=where, device_id_type=MESH)

    @pl.when(is_root)
    def _():
        def next_to(c):
            c = lax.rem(2 * columns - c + column, columns)
            return {"ia": c // nj, "ja": lax.rem(c, nj)}

        @pl.loop(0, columns)
        def _(c):
            greet({**next_to(c), "ka": 0})

        @pl.when(serves > 0)
        def _():
            @pl.loop(1, columns)
            def _(c):
                greet({**next_to(c), "ka": serves})

            pl.when(other_root)(functools.partial(greet, {"ka": serves}))

    beside = [
        (ia > 0, {"ia": jnp.maximum(ia - 1, 0)}),
        (ia < ni - 1, {"ia": jnp.minimum(ia + 1, ni - 1)}),
        (ja > 0, {"ja": jnp.maximum(ja - 1, 0)}),
        (ja < nj - 1, {"ja": jnp.minimum(ja + 1, nj - 1)}),
    ]
    expected = jnp.where(own_root, 0, 1) + jnp.where(ka == 0, nk - 1, 0)
    for (below, _), (above, where) in (beside[0:2], beside[2:4]):
        pl.when(above)(functools.partial(greet, where))
        expected = expected + below.astype(jnp.int32)
    lead = nk // 2
    leads = ka == lead
    pl.when(~leads)(functools.partial(greet, {"ka": lead}))
    expected = expected + jnp.where(leads, nk - 1, 0)

    lane = lax.broadcasted_iota(jnp.int32, (8, 128), 1)

    in_shapes.wait()
    in_mask.wait()
    in_coords.wait()
    packed = jnp.zeros((modes, 128), jnp.float32)
    disp = jnp.zeros((li, lj), jnp.float32)
    speed = jnp.zeros((li, lj), jnp.float32)
    zeros = jnp.zeros((modes, 128 - lj), jnp.float32)
    for i in range(li):
        wide = jnp.concatenate([sv[:, i, :], zeros], axis=1)
        packed = packed + (pltpu.roll(wide, lj * i, 1) if i else wide)
    for m in range(modes):
        one = sv[m]
        disp = disp + coords[0, ka * modes + m] * one
        speed = speed + coords[1, ka * modes + m] * one
    s_own[...] = packed
    planes[...] = jnp.concatenate([disp, speed, jnp.zeros((li, 128 - 2 * lj), jnp.float32)], axis=1)

    pl.when(expected > 0)(functools.partial(pl.semaphore_wait, barrier, expected))
    for axis, (there, where) in enumerate((beside[0], beside[2])):

        @pl.when(there)
        def _(axis=axis, where=where):
            pl.semaphore_signal(edge_sem.at[axis], inc=1, device_id=where, device_id_type=MESH)

    @pl.when(leads)
    def _():
        for o in range(1, nk):
            pl.semaphore_signal(
                column_sem, inc=1, device_id={"ka": lax.rem(ka + o, nk)}, device_id_type=MESH
            )

    def to_root(src, dst, sem_index, recv, where):
        return pltpu.make_async_remote_copy(
            src_ref=src, dst_ref=dst, send_sem=send_sem.at[sem_index], recv_sem=recv,
            device_id=where, device_id_type=MESH,
        )

    slots = [lax.rem(column - i * nj + columns, columns) for i, _ in root_of]
    load_copies = [
        to_root(l_own, l_all.at[slots[o]], 8 + o, many_sem.at[1], {"ia": root_of[o][0], "ja": 0, "ka": root_of[o][1]})
        for o in range(nk)
    ]
    slot = jnp.where(odd, slots[1], slots[0])
    shape_copy = to_root(s_own, s_all.at[slot], 7, many_sem.at[0], {"ia": root_ia, "ja": 0, "ka": root_ka})

    pl.when(~own_root)(shape_copy.start)

    in_flow.wait()

    @pl.when(ka == 0)
    def _():
        lane_t = lax.broadcasted_iota(jnp.int32, (lj, 128), 1)
        turned = jnp.zeros((lj, 128), jnp.float32)
        for i in range(li):
            p = primitives([fv[i, c, :, 0:1] for c in range(5)])[4]
            turned = turned + jnp.where(lax.rem(lane_t, li) == i, p - FAR_PRESSURE, 0.0)
        flat = jnp.concatenate([turned] * (128 // lj), axis=0).T[0:li]
        keep = jnp.concatenate([mv[...]] * (128 // lj), axis=1)
        own_row = lane // lj == lax.broadcasted_iota(jnp.int32, (8, 128), 0)
        l_own[...] = jnp.sum(jnp.where(own_row & (keep == 1), flat, 0.0), axis=0, keepdims=True)

    @pl.when(ka == 0)
    def _():
        for copy in load_copies:
            copy.start()

    @pl.when(own_root)
    def _():
        s_all[0] = s_own[...]

    def halo(src, dst, index, where):
        return pltpu.make_async_remote_copy(
            src_ref=src, dst_ref=dst, send_sem=send_sem.at[index], recv_sem=recv_sem.at[index],
            device_id=where, device_id_type=MESH,
        )

    (has_i0, to_i0), (has_i1, to_i1), (has_j0, to_j0), (has_j1, to_j1) = beside
    has_k0, has_k1 = ka > 0, ka < nk - 1
    copies = [
        (halo(flow.at[li - 2 : li], raw_i.at[0], 0, to_i1), has_i1, has_i0),
        (halo(flow.at[0:2], raw_i.at[1], 1, to_i0), has_i0, has_i1),
        (halo(flow.at[:, :, lj - 2 : lj], raw_j.at[0, :, :, 6:8], 2, to_j1), has_j1, has_j0),
        (halo(flow.at[:, :, 0:2], raw_j.at[1, :, :, 0:2], 3, to_j0), has_j0, has_j1),
        (halo(send_k.at[0], halo_k.at[0], 4, {"ka": jnp.minimum(ka + 1, nk - 1)}), has_k1, has_k0),
        (halo(send_k.at[1], halo_k.at[1], 5, {"ka": jnp.maximum(ka - 1, 0)}), has_k0, has_k1),
    ]
    for copy, sends, _ in (copies[1], copies[3]):
        pl.when(sends)(copy.start)

    plane_copies = [
        pltpu.make_async_remote_copy(
            src_ref=planes, dst_ref=planes_in.at[o - 1], send_sem=send_sem.at[15 + o],
            recv_sem=many_sem.at[2], device_id={"ka": lax.rem(ka + o, nk)}, device_id_type=MESH,
        )
        for o in range(1, nk)
    ]
    lane_j = lax.broadcasted_iota(jnp.int32, (lj, 128), 1)
    send_k[...] = jnp.zeros_like(send_k)

    @pl.loop(0, li)
    def _(i):
        here = lane_j // 2 == i
        for c, w in enumerate(primitives([fv[i, c] for c in range(5)])):
            prim[i + 2, c, 8 : 8 + lj] = w
            send_k[0, c] = jnp.where(here, pltpu.roll(w, 2 * i + 2, 1), send_k[0, c])
            send_k[1, c] = jnp.where(here, pltpu.roll(w, 2 * i, 1), send_k[1, c])

    def far(shape, c):
        return jnp.full(shape, FAR_STATE[c], jnp.float32)

    for base, (_, _, gets) in zip((0, li + 2), copies[0:2]):

        @pl.when(~gets)
        def _(base=base):
            for r in range(2):
                for c in range(5):
                    prim[base + r, c, 8 : 8 + lj] = far((lj, lk), c)

    for base, (_, _, gets) in zip((0, 8 + lj), copies[2:4]):

        @pl.when(~gets)
        def _(base=base):
            @pl.loop(0, li)
            def _(i):
                for c in range(5):
                    prim[i + 2, c, base : base + 8] = far((8, lk), c)

    @pl.when(~has_k0)
    def _():
        halo_k[0] = jnp.zeros(halo_k.shape[1:], jnp.float32)

    @pl.when(~has_k1)
    def _():
        for c in range(5):
            halo_k[1, c] = far((lj, 128), c)

    pl.when(~leads)(functools.partial(pl.semaphore_wait, column_sem, 1))
    for copy in plane_copies:
        copy.start()
    for copy, sends, _ in copies[4:6]:
        pl.when(sends)(copy.start)
    for axis, (copy, sends, _) in ((1, copies[2]), (0, copies[0])):

        @pl.when(sends)
        def _(axis=axis, copy=copy):
            pl.semaphore_wait(edge_sem.at[axis], 1)
            copy.start()

    pltpu.make_async_copy(planes_in, planes_in, many_sem.at[2]).wait()
    total = planes[...]
    for o in range(nk - 1):
        total = total + planes_in[o]
    wall = mv[...].astype(jnp.float32)
    wall = jnp.concatenate([jnp.zeros((li, 2 * lj), jnp.float32), wall, jnp.zeros((li, 128 - 3 * lj), jnp.float32)], axis=1)
    turned = jnp.concatenate([total + wall, jnp.zeros((128 - li, 128), jnp.float32)], axis=0).T

    for side, (base, (copy, _, gets)) in enumerate(zip((0, 8 + lj), copies[2:4])):

        @pl.when(gets)
        def _(side=side, base=base, copy=copy):
            copy.wait_recv()

            @pl.loop(0, li)
            def _(i):
                for c, w in enumerate(primitives([raw_j[side, i, c] for c in range(5)])):
                    prim[i + 2, c, base : base + 8] = w

    pl.when(has_k0)(copies[4][0].wait_recv)
    pl.when(has_k1)(copies[5][0].wait_recv)

    first = ka * lk
    own_pair = [send_k[0, c] for c in range(5)]
    next_pair = [halo_k[1, c] for c in range(5)]
    last_weight = (1.0 - (first + lk).astype(jnp.float32) / total_k) ** 2
    speed_pairs = jnp.zeros((lj, 128), jnp.float32)
    for i in range(li):
        speed_pairs = jnp.where(lane_j // 2 == i, turned[lj : 2 * lj, i : i + 1], speed_pairs)
    last = faces(
        own_pair,
        [pltpu.roll(w, 127, 1) for w in own_pair],
        next_pair,
        [pltpu.roll(w, 127, 1) for w in next_pair],
        3,
        last_weight * speed_pairs,
    )
    for c in range(5):
        edge_k[c] = last[c]

    def cells(i, lo, rows):
        return [prim[i, c, lo : lo + rows] for c in range(5)]

    def along_i(i):
        return faces(cells(i, 8, lj), cells(i + 1, 8, lj), cells(i + 2, 8, lj), cells(i + 3, 8, lj), 1)

    at_wall = ka == 0
    lane_f = (first + lane_j).astype(jnp.float32)
    face_weight = (1.0 - lane_f / total_k) ** 2
    cell_weight = STRAIN * (1.0 - (lane_f + 0.5) / total_k)
    first_lane, pair_lane, last_lane = lane_j < 1, lane_j < 2, lane_j == lk - 1
    column_lane = lax.broadcasted_iota(jnp.int32, (3 * lj, 128), 1)

    @pl.loop(0, li)
    def _(n):
        i = jnp.where(n < li - 4, n + 2, jnp.where(n < li - 2, n - (li - 4), n))
        for side, (turn, base) in enumerate(((li - 4, 0), (li - 2, li + 2))):

            @pl.when((n == turn) & copies[side][2])
            def _(side=side, base=base):
                copies[side][0].wait_recv()
                for r in range(2):
                    for c, w in enumerate(primitives([raw_i[side, r, c] for c in range(5)])):
                        prim[base + r, c, 8 : 8 + lj] = w

        @pl.when((n == 0) | (n == li - 4) | (n == li - 2))
        def _():
            for c, w in enumerate(along_i(i)):
                flux_i[c] = w

        column_i = jnp.sum(jnp.where(column_lane == i, turned[0 : 3 * lj], 0.0), axis=1, keepdims=True)
        disp_i = column_i[0:lj]
        speed_i = jnp.broadcast_to(column_i[lj : 2 * lj], (lj, 128))
        solid = jnp.broadcast_to(column_i[2 * lj : 3 * lj], (lj, 128)) > 0.5

        upper = along_i(i + 1)
        residual = []
        for c in range(5):
            residual.append(upper[c] - flux_i[c])
            flux_i[c] = upper[c]

        rows = lj + 8
        flux_j = faces(cells(i + 2, 6, rows), cells(i + 2, 7, rows), cells(i + 2, 8, rows), cells(i + 2, 9, rows), 2)
        residual = [r + (f[1 : lj + 1] - f[0:lj]) for r, f in zip(residual, flux_j)]

        below2, below, above = [], [], []
        own = cells(i + 2, 8, lj)
        for c, w in enumerate(own):
            up = jnp.where(last_lane, pltpu.roll(halo_k[1, c], lk - 1 - 2 * i, 1), pltpu.roll(w, lk - 1, 1))
            down = pltpu.roll(w, 1, 1)
            mirror2 = jnp.where(first_lane, up, down)
            mirror1 = w
            if c == 3:
                mirror2 = 2.0 * speed_i - mirror2
                mirror1 = 2.0 * speed_i - mirror1
            mirror2 = jnp.where(solid, mirror2, FAR_STATE[c])
            mirror1 = jnp.where(solid, mirror1, FAR_STATE[c])
            ghost = halo_k[0, c]
            ghost2 = jnp.where(at_wall, mirror2, pltpu.roll(ghost, lax.rem(lk - 2 * i, lk), 1))
            ghost1 = jnp.where(at_wall, mirror1, pltpu.roll(ghost, lk - 1 - 2 * i, 1))
            below2.append(jnp.where(pair_lane, ghost2, pltpu.roll(w, 2, 1)))
            below.append(jnp.where(first_lane, ghost1, down))
            above.append(up)
        flux_k = faces(below2, below, own, above, 3, face_weight * speed_i)
        growth = (-0.5 * SECTION_STEP) * jnp.exp(cell_weight * disp_i)
        for c, f in enumerate(flux_k):
            end = pltpu.roll(edge_k[c], lk - 1 - 2 * i, 1)
            high = jnp.where(last_lane, end, pltpu.roll(f, lk - 1, 1))
            new[i, c] = fv[i, c] + growth * (residual[c] + (high - f))

    for copy, sends, _ in copies:
        pl.when(sends)(copy.wait_send)
    for copy in plane_copies:
        copy.wait_send()
    pl.when(~own_root)(shape_copy.wait_send)

    @pl.when(ka == 0)
    def _():
        for copy in load_copies:
            copy.wait_send()

    near = min(4, nj)
    line = lax.rem(ia, lines)
    order = [o % lines for o in (7, 4, 6, 5, 1, 3, 2, 0)][:lines] if lines == 8 else list(range(lines))
    direct = [
        {"ia": lax.rem(ia + o, lines), "ja": j, "ka": serves}
        for j in range(near)
        for o in order
        if j or o
    ]
    passed = [
        {"ia": line + lines * h, "ja": j}
        for h in range(ni // lines)
        for j in range(nj)
        if h or j >= near
    ]
    hands_on = (ia < lines) & (ja == near - 1)

    def give(source, targets):
        for where in targets:
            pltpu.make_async_remote_copy(
                src_ref=source, dst_ref=g_own, send_sem=many_sem.at[4], recv_sem=many_sem.at[3],
                device_id=where, device_id_type=MESH,
            ).start()

    def sent(targets):
        if targets:
            left = l_all.at[0 : len(targets)]
            pltpu.make_async_copy(left, left, many_sem.at[4]).wait()

    @pl.when(is_root)
    def _():
        @pl.when(own_root)
        def _():
            others = s_all.at[1:columns]
            pltpu.make_async_copy(others, others, many_sem.at[0]).wait()

        @pl.when(other_root)
        def _():
            pltpu.make_async_copy(s_all, s_all, many_sem.at[0]).wait()

        pltpu.make_async_copy(l_all, l_all, many_sem.at[1]).wait()
        summed = jnp.sum(s_all[...] * l_all[...], axis=0)
        each = jnp.sum(summed, axis=1, keepdims=True)
        row = lax.broadcasted_iota(jnp.int32, (8, 128), 0)
        g_sum[...] = jnp.sum(jnp.where(lane == row, each, 0.0), axis=0, keepdims=True)
        give(g_sum, direct)
        beside_core = [{"ka": serves}]

        @pl.when(other_root)
        def _():
            give(g_sum, beside_core)
            sent(direct + beside_core)

        @pl.when(own_root)
        def _():
            force[...] = g_sum[...]
            sent(direct)

    @pl.when(~own_root)
    def _():
        pltpu.make_async_copy(g_own, g_own, many_sem.at[3]).wait()
        pl.when(hands_on)(functools.partial(give, g_own, passed))
        force[...] = g_own[...]
        pl.when(hands_on)(functools.partial(sent, passed))


def finish(scale, new, partial, out, force, sem):
    copy = pltpu.make_async_copy(new, out, sem)
    copy.start()
    force[...] = partial[:, 0 : force.shape[1]] * scale
    copy.wait()


def solution(mesh):
    sizes = (mesh.shape["ia"], mesh.shape["ja"], mesh.shape["ka"])
    ni, nj, nk = sizes

    def local(flow_state, mode_shapes, modal_coords, wall_mask):
        li, _, lj, lk = flow_state.shape
        modes = mode_shapes.shape[0]
        f32 = jnp.float32
        tile = pltpu.VMEM((8, 128), f32)
        row = pltpu.VMEM((1, 128), f32)
        vmem = pl.BlockSpec(memory_space=pltpu.VMEM)
        hbm = pl.BlockSpec(memory_space=pltpu.HBM)
        held = functools.partial(pltpu.with_memory_space_constraint, memory_space=pltpu.HBM)
        new, partial = pl.pallas_call(
            functools.partial(section, sizes),
            out_shape=(pltpu.VMEM(flow_state.shape, f32), pltpu.VMEM((1, 128), f32)),
            in_specs=[hbm, hbm, hbm, hbm],
            out_specs=(vmem, vmem),
            scratch_shapes=[
                pltpu.VMEM(flow_state.shape, f32),
                pltpu.VMEM(mode_shapes.shape, f32),
                pltpu.VMEM(wall_mask.shape, jnp.int32),
                pltpu.SMEM(modal_coords.shape, f32),
                pltpu.VMEM((li + 4, 5, lj + 24, lk), f32),
                pltpu.VMEM((2, 2, 5, lj, lk), f32),
                pltpu.VMEM((2, li, 5, 8, lk), f32),
                pltpu.VMEM((2, 5, lj, 128), f32),
                pltpu.VMEM((2, 5, lj, 128), f32),
                pltpu.VMEM((5, lj, 128), f32),
                tile,
                pltpu.VMEM((nk - 1, 8, 128), f32),
                tile,
                row,
                pltpu.VMEM((ni * nj, 8, 128), f32),
                pltpu.VMEM((ni * nj, 1, 128), f32),
                row,
                row,
                pltpu.VMEM((5, lj, lk), f32),
                pltpu.SemaphoreType.DMA((4,)),
                pltpu.SemaphoreType.DMA((15 + nk,)),
                pltpu.SemaphoreType.DMA((6,)),
                pltpu.SemaphoreType.DMA((5,)),
                pltpu.SemaphoreType.REGULAR,
                pltpu.SemaphoreType.REGULAR((2,)),
            ],
            compiler_params=pltpu.CompilerParams(
                collective_id=0, has_side_effects=True, vmem_limit_bytes=32 * 1024 * 1024
            ),
            name="section",
        )(held(flow_state), held(mode_shapes), held(modal_coords), held(wall_mask))
        out, force = pl.pallas_call(
            functools.partial(finish, 1.0 / math.sqrt(ni * li * nj * lj)),
            out_shape=(
                jax.ShapeDtypeStruct(flow_state.shape, f32),
                jax.ShapeDtypeStruct((1, modes), f32),
            ),
            in_specs=[vmem, vmem],
            out_specs=(hbm, vmem),
            scratch_shapes=[pltpu.SemaphoreType.DMA],
            compiler_params=pltpu.CompilerParams(vmem_limit_bytes=8 * 1024 * 1024),
            name="finish",
        )(new, partial)
        return (out, force.reshape(modes))

    return jax.shard_map(
        local,
        mesh=mesh,
        in_specs=(P("ia", None, "ja", "ka"), P("ka", "ia", "ja"), P(), P("ia", "ja")),
        out_specs=(P("ia", None, "ja", "ka"), P("ka")),
        check_vma=False,
    )
```
